128 devices in a mesh: gz: 16 (over x_lo, y, core), gy: 8 (over x_hi, z).
Axes of the slice: x: 4 (x_hi: 2, x_lo: 2; x = x_hi * 2 + x_lo), y: 4, z: 4, core: 2. Of those that a mesh axis runs over, the one named last changes fastest.
Arguments:
- air_now: float32 [128, 1024, 1024], P('gz', 'gy'), may hold values from -6 to 6
- air_prev: float32 [128, 1024, 1024], P('gz', 'gy'), may hold values from -6 to 6
- plate_now: float32 [2048, 4096], P(('gz', 'gy')), may hold values from -6 to 6
- plate_prev: float32 [2048, 4096], P(('gz', 'gy')), may hold values from -6 to 6
- plate_level: int32 [1], replicated, may hold values from 0 to 126
- plate_shift: int32 [1], replicated, may hold values from 0 to 512
Outputs:
- air_field: float32 [128, 1024, 1024], P('gz', 'gy')
- plate_field: float32 [2048, 4096], P(('gz', 'gy'))
The draws below stay inside these ranges and needn't reach their ends.
Inputs may be any that keep to these rules, and one draw needn't show every extreme that they name: plate_level[0] and plate_level[0] + 1 are both air levels. The plate's footprint, rows plate_shift[0] to plate_shift[0] + 511, lies inside the air box.
All inputs are finite; a program needn't handle non-finite values.
Results may differ from the reference program's by a relative error of at most 0.0001.
Values sent between devices are 32-bit elements; how exact they have to be, the bound alone decides.
No kernel may reach another device: no remote copies, remote signals or barrier semaphores. Data moves between devices by JAX's collectives and lax.ppermute only.
A program may use at most 128 MiB of HBM per device.

```python
import jax
import jax.numpy as jnp
from jax import lax

NXA = 1024
STEPS = 2
NZ = 128
NY = 1024
PROWS = 2048
PCOLS = 4096
FOOT_ROWS = 512


def block_scale(rng, dims, pieces, low, largest):
    def one(axis_at, blocks):
        heights = jax.random.uniform(jax.random.fold_in(jax.random.fold_in(rng, 6), axis_at), (blocks,), jnp.float32, low / len(pieces), largest / len(pieces))
        return jnp.repeat(jnp.exp(heights), dims[axis_at] // blocks).reshape((-1,) + (1,) * (len(dims) - axis_at - 1))

    gain = one(*pieces[0])
    for cut in pieces[1:]:
        gain = gain * one(*cut)
    return gain


def gaussian(stream_key, extent, spread, limit, shards=(), held_as=jnp.bfloat16):
    gain = block_scale(stream_key, extent, shards, -0.22, 0.18) if shards else 1.0
    values = jax.random.normal(stream_key, extent, jnp.float32) * spread * gain
    return jnp.minimum(jnp.maximum(values, -limit), limit).astype(held_as)


def setup_inputs(seed: int = 0) -> dict:
    keys = jax.random.split(jax.random.key(seed), 7)
    return {
        "air_now": gaussian(keys[0], (NZ, NY, NXA), 1.0, 6.0, ((0, 16), (1, 8)), jnp.float32),
        "air_prev": gaussian(keys[1], (NZ, NY, NXA), 1.0, 6.0, ((0, 16), (1, 8)), jnp.float32),
        "plate_now": gaussian(keys[2], (PROWS, PCOLS), 1.0, 6.0, ((0, 128),), jnp.float32),
        "plate_prev": gaussian(keys[3], (PROWS, PCOLS), 1.0, 6.0, ((0, 128),), jnp.float32),
        "plate_level": jax.random.randint(keys[4], (1,), 0, NZ - 1).astype(jnp.int32),
        "plate_shift": jax.random.randint(keys[5], (1,), 0, NY - FOOT_ROWS + 1).astype(jnp.int32),
    }


def air_laplace(field):
    padded = jnp.pad(field, 1)
    beside_all = padded[2:, 1:-1, 1:-1] + padded[:-2, 1:-1, 1:-1]
    beside_all = beside_all + padded[1:-1, 2:, 1:-1] + padded[1:-1, :-2, 1:-1]
    beside_all = beside_all + padded[1:-1, 1:-1, 2:] + padded[1:-1, 1:-1, :-2]
    return beside_all - 6.0 * field


def plate_laplace(field):
    padded = jnp.pad(field, 1)
    beside_all = padded[2:, 1:-1] + padded[:-2, 1:-1] + padded[1:-1, 2:] + padded[1:-1, :-2]
    return beside_all - 4.0 * field


def reference(air_now, air_prev, plate_now, plate_prev, plate_level, plate_shift):
    level = plate_level[0].astype(jnp.int32)
    shift = plate_shift[0].astype(jnp.int32)
    levels = jnp.arange(NZ, dtype=jnp.int32)
    select = (levels == level).astype(jnp.float32) - (levels == level + 1).astype(jnp.float32)
    for step in range(STEPS):
        upper = lax.dynamic_index_in_dim(air_now, level + 1, 0, keepdims=False)
        lower = lax.dynamic_index_in_dim(air_now, level, 0, keepdims=False)
        plane = upper - lower
        pressure = lax.dynamic_slice_in_dim(plane, shift, FOOT_ROWS, 0)
        force = jnp.repeat(jnp.repeat(pressure, 4, 0), 4, 1)
        motion = (plate_now - plate_prev).reshape(FOOT_ROWS, 4, NXA, 4).mean(axis=(1, 3))
        source = lax.dynamic_update_slice_in_dim(jnp.zeros((NY, NXA), jnp.float32), motion, shift, 0)
        air_next = 2.0 * air_now - air_prev + 0.3 * air_laplace(air_now)
        air_next = air_next + 0.5 * source[None] * select[:, None, None]
        bend = plate_laplace(plate_laplace(plate_now))
        plate_next = (2.0 * plate_now - 0.99 * plate_prev - 0.04 * bend + 0.5 * force) / 1.01
        air_prev, air_now = air_now, air_next
        plate_prev, plate_now = plate_now, plate_next
    return air_now, plate_now
```

```python
import functools

import jax
import jax.numpy as jnp
from jax import lax
from jax.experimental import pallas as pl
from jax.experimental.pallas import tpu as pltpu
from jax.sharding import PartitionSpec as P

F32 = jnp.float32
C_PRESS = 0.5 / 1.01
HIGH = lax.Precision.HIGHEST


def params(mib):
    return pltpu.CompilerParams(vmem_limit_bytes=mib << 20)


def cost(nbytes):
    return pl.CostEstimate(flops=nbytes, bytes_accessed=nbytes, transcendentals=0)


def iota(shape, axis):
    return lax.broadcasted_iota(jnp.int32, shape, axis)


def left_right(x):
    width = x.shape[1]
    col = iota(x.shape, 1)
    west = jnp.where(col == 0, 0.0, pltpu.roll(x, 1, 1))
    east = jnp.where(col == width - 1, 0.0, pltpu.roll(x, width - 1, 1))
    return west + east


def up_down(x, above, below):
    height = x.shape[0]
    row = iota(x.shape, 0)
    up = jnp.where(row == 0, above, pltpu.roll(x, 1, 0))
    down = jnp.where(row == height - 1, below, pltpu.roll(x, height - 1, 0))
    return up + down


def air_kernel(now, prev, zlo, zhi, ylo, yhi, out, *edges):
    z = pl.program_id(0)
    depth = now.shape[0]
    here = now[z]
    under = jnp.where(z == 0, zlo[...], now[jnp.maximum(z - 1, 0)])
    over = jnp.where(z == depth - 1, zhi[...], now[jnp.minimum(z + 1, depth - 1)])
    total = under + over + left_right(here)
    total = total + up_down(here, ylo[pl.ds(z, 1), :], yhi[pl.ds(z, 1), :])
    nxt = 0.2 * here - prev[0] + 0.3 * total
    out[0] = nxt
    if edges:
        height = here.shape[0]
        edges[0][pl.ds(z, 1), :] = nxt[0:1]
        edges[1][pl.ds(z, 1), :] = nxt[height - 1 : height]


def air_step(now, prev, zlo, zhi, ylo, yhi, want_edges):
    depth, height, width = now.shape
    plane = pl.BlockSpec((1, height, width), lambda z: (z, 0, 0))
    face = pl.BlockSpec((height, width), lambda z: (0, 0))
    rows = pl.BlockSpec((depth, width), lambda z: (0, 0))
    out_shape = [jax.ShapeDtypeStruct(now.shape, F32)]
    out_specs = [plane]
    if want_edges:
        out_shape += [jax.ShapeDtypeStruct((depth, width), F32)] * 2
        out_specs += [rows, rows]
    return pl.pallas_call(
        air_kernel,
        grid=(depth,),
        in_specs=[
            pl.BlockSpec((depth, height, width), lambda z: (0, 0, 0)),
            plane,
            face,
            face,
            rows,
            rows,
        ],
        out_specs=out_specs,
        out_shape=out_shape,
        compiler_params=params(30),
        cost_estimate=cost(14 << 20),
    )(now, prev, zlo, zhi, ylo, yhi)


def press_kernel(scal, up2, up1, at0, dn1, pup1, pat0, ylo, yhi, out, c0, c1):
    level, shift, base = scal[0], scal[1], scal[2]
    depth = ylo.shape[0]
    height, width = c0.shape

    def mine(z):
        return jnp.where((z >= base) & (z < base + depth), 1.0, 0.0).astype(F32)

    here = (level + 2 >= base) & (level - 1 < base + depth)

    @pl.when(jnp.logical_not(here))
    def _():
        out[...] = jnp.zeros(out.shape, F32)

    @pl.when(here)
    def _():
        m1, m0 = mine(level + 1), mine(level)
        m2, mm = mine(level + 2), mine(level - 1)
        z = iota((depth, width), 0) + base
        pick = jnp.where(z == level + 1, 1.0, 0.0) - jnp.where(z == level, 1.0, 0.0)
        above = jnp.sum(pick * ylo[...], axis=0, keepdims=True)
        below = jnp.sum(pick * yhi[...], axis=0, keepdims=True)
        top, bottom = m1 * up1[0], m0 * at0[0]
        press = top - bottom
        flat = left_right(press) + up_down(press, above, below) - 4.0 * press
        vertical = m2 * up2[0] - 3.0 * press - mm * dn1[0]
        older = m1 * pup1[0] - m0 * pat0[0]
        c0[...] = press
        c1[...] = 2.0 * press - older + 0.3 * (flat + vertical)
        b = shift & 31
        turn = (32 - b) & 31
        for k in range(height // 32):
            r0 = pltpu.roll(c0[32 * k : 32 * k + 32], turn, 0)
            r1 = pltpu.roll(c1[32 * k : 32 * k + 32], turn, 0)
            for y in range(8):
                out[y, 8 * k : 8 * k + 4, :] = r0[4 * y : 4 * y + 4]
                out[y, 8 * k + 4 : 8 * k + 8, :] = r1[4 * y : 4 * y + 4]


def press_pack(scal, air_now, air_prev, ylo, yhi):
    depth, height, width = air_now.shape

    def plane(offset):
        def where(i, scal):
            return (jnp.clip(scal[0] + offset - scal[2], 0, depth - 1), 0, 0)

        return pl.BlockSpec((1, height, width), where)

    rows = pl.BlockSpec((depth, width), lambda i, scal: (0, 0))
    return pl.pallas_call(
        press_kernel,
        grid_spec=pltpu.PrefetchScalarGridSpec(
            num_scalar_prefetch=1,
            grid=(1,),
            in_specs=[plane(2), plane(1), plane(0), plane(-1), plane(1), plane(0), rows, rows],
            out_specs=pl.BlockSpec((8, 32, width), lambda i, scal: (0, 0, 0)),
            scratch_shapes=[pltpu.VMEM((height, width), F32)] * 2,
        ),
        out_shape=jax.ShapeDtypeStruct((8, 32, width), F32),
        compiler_params=params(30),
        cost_estimate=cost(4 << 20),
    )(scal, air_now, air_now, air_now, air_now, air_prev, air_prev, ylo, yhi)


def flat_laplace(x):
    height = x.shape[0]
    return left_right(x) + pltpu.roll(x, 1, 0) + pltpu.roll(x, height - 1, 0) - 4.0 * x


def inside_rows(shape, first, last_row):
    row = iota(shape, 0) + first
    return (row >= 0) & (row < last_row)


def plate_kernel(n_rows, scal, now, prev, lo, hi, next_ext, motion):
    rows, cols = now.shape
    first = scal[3] * rows - 4
    here = now[...]
    ext = jnp.concatenate([lo[0:4], here, hi[0:4]], axis=0)
    old = jnp.concatenate([lo[4:8], prev[...], hi[4:8]], axis=0)
    ok = inside_rows(ext.shape, first, n_rows)
    inner = jnp.where(ok, flat_laplace(ext), 0.0)
    bend = flat_laplace(inner)
    nxt = (2.0 * ext - 0.99 * old - 0.04 * bend) * (1.0 / 1.01)
    nxt = jnp.where(ok, nxt, 0.0)
    next_ext[...] = nxt
    both = jnp.concatenate([here - prev[...], nxt[4 : 4 + rows] - here], axis=0)
    fold = jnp.where((iota((512, 128), 0) >> 2) == iota((512, 128), 1), 1.0, 0.0)
    parts = [
        jnp.dot(both[:, 512 * q : 512 * q + 512], fold, precision=HIGH, preferred_element_type=F32)
        for q in range(cols // 512)
    ]
    narrow = jnp.concatenate(parts, axis=1)
    pick = jnp.where(iota((8, 32), 0) == (iota((8, 32), 1) >> 2), 1.0 / 16.0, 0.0)
    motion[...] = jnp.dot(pick, narrow, precision=HIGH, preferred_element_type=F32)


def plate_first(scal, now, prev, lo, hi, n_rows):
    rows, cols = now.shape
    return pl.pallas_call(
        functools.partial(plate_kernel, n_rows),
        in_specs=[pl.BlockSpec(memory_space=pltpu.SMEM)]
        + [pl.BlockSpec(memory_space=pltpu.VMEM)] * 4,
        out_specs=[pl.BlockSpec(memory_space=pltpu.VMEM)] * 2,
        out_shape=[
            jax.ShapeDtypeStruct((rows + 8, cols), F32),
            jax.ShapeDtypeStruct((8, cols // 4), F32),
        ],
        compiler_params=params(16),
        cost_estimate=cost(4 << 20),
    )(scal, now, prev, lo, hi)


def carries(shape, strip, b):
    return (4 * strip + (iota(shape, 0) & 3) + b) >= 32


def to_plate_kernel(scal, came, motion, out):
    shift, strip = scal[1], scal[4]
    a, b = shift >> 5, shift & 31
    move = motion[...]
    carry = carries(move.shape, strip, b)
    for dest in range(16):
        at = pl.multiple_of(8 * (dest + a), 8)
        after = pl.multiple_of(8 * jnp.minimum(dest + a + 1, 31), 8)
        out[dest, 0:8, :] = jnp.where(carry, came[pl.ds(after, 8), :], came[pl.ds(at, 8), :])
        out[dest, 8:16, :] = move


def to_plate(scal, came, motion):
    width = motion.shape[1]
    return pl.pallas_call(
        to_plate_kernel,
        in_specs=[pl.BlockSpec(memory_space=pltpu.SMEM)]
        + [pl.BlockSpec(memory_space=pltpu.VMEM)] * 2,
        out_specs=pl.BlockSpec(memory_space=pltpu.VMEM),
        out_shape=jax.ShapeDtypeStruct((16, 16, width), F32),
        compiler_params=params(16),
        cost_estimate=cost(2 << 20),
    )(scal, came, motion)


def to_air_kernel(scal, came, pressure, out):
    shift, strip = scal[1], scal[4]
    a, b = shift >> 5, shift & 31
    width = pressure.shape[1]
    total = came[0, 0:8, :]
    for src in range(1, 16):
        total = total + came[src, 0:8, :]
    pressure[...] = total
    shape = (8, width)
    carry = carries(shape, strip, b)
    row = iota(shape, 0)
    place = (4 * strip + (row & 3) + b) & 31
    first_field = row < 4

    def tile(block):
        def one(src):
            ok = jnp.where((src >= 0) & (src < 16), 1.0, 0.0).astype(F32)
            return came[jnp.clip(src, 0, 15), 8:16, :] * ok

        return jnp.where(carry, one(block - a - 1), one(block - a))

    for s in range(8):
        tiles = [tile(4 * s + k) for k in range(4)]
        for k in range(4):
            out[s, 8 * k : 8 * k + 8, :] = tiles[k]
        if s > 0:
            before = jnp.where(first_field & (place == 31), tile(4 * s - 1), 0.0)
        else:
            before = jnp.zeros(shape, F32)
        if s < 7:
            behind = jnp.where(first_field & (place == 0), tile(4 * s + 4), 0.0)
        else:
            behind = jnp.zeros(shape, F32)
        out[s, 32:40, :] = before + pltpu.roll(behind, 4, 0)


def to_air(scal, came):
    width = came.shape[2]
    return pl.pallas_call(
        to_air_kernel,
        in_specs=[
            pl.BlockSpec(memory_space=pltpu.SMEM),
            pl.BlockSpec(memory_space=pltpu.VMEM),
        ],
        out_specs=[pl.BlockSpec(memory_space=pltpu.VMEM)] * 2,
        out_shape=[
            jax.ShapeDtypeStruct((8, width), F32),
            jax.ShapeDtypeStruct((8, 40, width), F32),
        ],
        compiler_params=params(16),
        cost_estimate=cost(2 << 20),
    )(scal, came)


def local_press_kernel(scal, up1, at0, zlo, zhi, out):
    level, shift, base, strip = scal[0], scal[1], scal[2], scal[4]
    height, width = out.shape
    depth = 8
    top = jnp.where(level + 1 == base + depth, zhi[...], up1[0])
    bottom = jnp.where(level == base - 1, zlo[...], at0[0])
    y = iota((height, width), 0) + strip * height - shift
    out[...] = jnp.where((y >= 0) & (y < 512), (0.5 * C_PRESS) * (top - bottom), 0.0)


def local_press(scal, air_now, zlo, zhi):
    depth, height, width = air_now.shape

    def plane(offset):
        def where(i, scal):
            return (jnp.clip(scal[0] + offset - scal[2], 0, depth - 1), 0, 0)

        return pl.BlockSpec((1, height, width), where)

    face = pl.BlockSpec((height, width), lambda i, scal: (0, 0))
    return pl.pallas_call(
        local_press_kernel,
        grid_spec=pltpu.PrefetchScalarGridSpec(
            num_scalar_prefetch=1,
            grid=(1,),
            in_specs=[plane(1), plane(0), face, face],
            out_specs=face,
        ),
        out_shape=jax.ShapeDtypeStruct((height, width), F32),
        compiler_params=params(16),
        cost_estimate=cost(2 << 20),
    )(scal, air_now, air_now, zlo, zhi)


def force_kernel(scal, field, came, press, out, q, r):
    level, shift, base = scal[0], scal[1], scal[2]
    t = pl.program_id(0)
    height, width = q.shape
    depth = 8
    b = shift & 31

    @pl.when(t == 0)
    def _():
        for k in range(height // 32):
            for f, ref in ((0, r), (1, q)):
                rows = [came[y, 8 * k + 4 * f : 8 * k + 4 * f + 4, :] for y in range(8)]
                ref[32 * k : 32 * k + 32, :] = pltpu.roll(jnp.concatenate(rows, axis=0), b, 0)
        rim = came[0, 32:40, :]
        for y in range(1, 8):
            rim = rim + came[y, 32:40, :]
        above = jnp.sum(rim[0:4], axis=0, keepdims=True)
        below = jnp.sum(rim[4:8], axis=0, keepdims=True)
        motion = r[...]
        around = left_right(motion) + up_down(motion, above, below)
        q[...] = (0.55 - 0.6) * motion + 0.15 * around + 0.5 * q[...] + press[...]

    z = jnp.clip(level - 1 + t - base, 0, depth - 1) + base

    def is_level(other):
        return jnp.where(z == other, 1.0, 0.0).astype(F32)

    wq = is_level(level) - is_level(level + 1)
    wr = 0.15 * (is_level(level - 1) - is_level(level + 2))
    out[0] = field[0] + wq * q[...] + wr * r[...]


def add_force(scal, field, came, press):
    depth, height, width = field.shape

    def where(t, scal):
        return (jnp.clip(scal[0] - 1 + t - scal[2], 0, depth - 1), 0, 0)

    plane = pl.BlockSpec((1, height, width), where)
    return pl.pallas_call(
        force_kernel,
        grid_spec=pltpu.PrefetchScalarGridSpec(
            num_scalar_prefetch=1,
            grid=(4,),
            in_specs=[
                plane,
                pl.BlockSpec((8, 40, width), lambda t, scal: (0, 0, 0)),
                pl.BlockSpec((height, width), lambda t, scal: (0, 0)),
            ],
            out_specs=plane,
            scratch_shapes=[pltpu.VMEM((height, width), F32)] * 2,
        ),
        out_shape=jax.ShapeDtypeStruct(field.shape, F32),
        input_output_aliases={1: 0},
        compiler_params=params(24),
        cost_estimate=cost(4 << 20),
    )(scal, field, came, press)


def plate_last_kernel(n_rows, scal, now, next_ext, pressure, motion, lo, hi, out):
    rows, cols = now.shape
    first = scal[3] * rows - 4
    own = pressure[...]
    width = own.shape[1]
    lines = jnp.concatenate(
        [own[0:4], own[4:8] - motion[0:4], lo[...], hi[...], jnp.zeros((6, width), F32)], axis=0
    )
    spread = jnp.where((iota((128, 512), 1) >> 2) == iota((128, 512), 0), 1.0, 0.0)
    parts = [
        jnp.dot(lines[:, 128 * q : 128 * q + 128], spread, precision=HIGH, preferred_element_type=F32)
        for q in range(width // 128)
    ]
    wide = jnp.concatenate(parts, axis=1)
    e = iota((24, 16), 0)
    line = iota((24, 16), 1)
    source = jnp.where(e < 4, 8, jnp.where(e >= 20, 9, (e - 4) >> 2))
    pick = jnp.where(line == source, C_PRESS, 0.0)
    push = jnp.dot(pick, wide, precision=HIGH, preferred_element_type=F32)
    pick = jnp.where(iota((16, 16), 1) == 4 + (iota((16, 16), 0) >> 2), C_PRESS, 0.0)
    push_last = jnp.dot(pick, wide, precision=HIGH, preferred_element_type=F32)
    ok = inside_rows(next_ext.shape, first, n_rows)
    mid = jnp.where(ok, next_ext[...] + push, 0.0)
    inner = jnp.where(ok, flat_laplace(mid), 0.0)
    bend = flat_laplace(inner)[4 : 4 + rows]
    final = (2.0 * mid[4 : 4 + rows] - 0.99 * now[...] - 0.04 * bend) * (1.0 / 1.01)
    out[...] = final + push_last


def plate_last(scal, now, next_ext, pressure, motion, lo, hi, n_rows):
    return pl.pallas_call(
        functools.partial(plate_last_kernel, n_rows),
        in_specs=[pl.BlockSpec(memory_space=pltpu.SMEM)]
        + [pl.BlockSpec(memory_space=pltpu.VMEM)] * 6,
        out_specs=pl.BlockSpec(memory_space=pltpu.VMEM),
        out_shape=jax.ShapeDtypeStruct(now.shape, F32),
        compiler_params=params(16),
        cost_estimate=cost(4 << 20),
    )(scal, now, next_ext, pressure, motion, lo, hi)


def neighbours(n):
    return [(i, i + 1) for i in range(n - 1)], [(i + 1, i) for i in range(n - 1)]


def shards(air_now, air_prev, plate_now, plate_prev, plate_level, plate_shift):
    depth, height, width = air_now.shape
    n_gz, n_gy = lax.axis_size("gz"), lax.axis_size("gy")
    slab, strip = lax.axis_index("gz"), lax.axis_index("gy")
    device = slab * n_gy + strip
    n_rows = plate_now.shape[0] * n_gz * n_gy
    zero = jnp.int32(0)
    scal = jnp.stack(
        [plate_level[0], plate_shift[0], slab * depth, device, strip, zero, zero, zero]
    ).astype(jnp.int32)
    up_y, down_y = neighbours(n_gy)
    up_z, down_z = neighbours(n_gz)
    up_d, down_d = neighbours(n_gz * n_gy)

    ylo = lax.ppermute(air_now[:, height - 1, :], "gy", up_y)
    yhi = lax.ppermute(air_now[:, 0, :], "gy", down_y)
    sent = press_pack(scal, air_now, air_prev, ylo, yhi)
    came = lax.all_to_all(sent, "gy", 0, 0).reshape(256, width)

    lo = jnp.concatenate([plate_now[-4:], plate_prev[-4:]], axis=0)
    hi = jnp.concatenate([plate_now[:4], plate_prev[:4]], axis=0)
    lo = lax.ppermute(lo, ("gz", "gy"), up_d)
    hi = lax.ppermute(hi, ("gz", "gy"), down_d)
    plate_ext, motion = plate_first(scal, plate_now, plate_prev, lo, hi, n_rows)

    zlo = lax.ppermute(air_now[depth - 1], "gz", up_z)
    zhi = lax.ppermute(air_now[0], "gz", down_z)
    air_1, first_rows, last_rows = air_step(air_now, air_prev, zlo, zhi, ylo, yhi, True)
    press_now = local_press(scal, air_now, zlo, zhi)
    ylo = lax.ppermute(last_rows, "gy", up_y)
    yhi = lax.ppermute(first_rows, "gy", down_y)
    zlo = lax.ppermute(air_1[depth - 1], "gz", up_z)
    zhi = lax.ppermute(air_1[0], "gz", down_z)
    (air_2,) = air_step(air_1, air_now, zlo, zhi, ylo, yhi, False)

    came = lax.all_to_all(to_plate(scal, came, motion), "gz", 0, 0)
    pressure, sent = to_air(scal, came)
    came = lax.all_to_all(sent, "gy", 0, 0)

    lo = lax.ppermute(pressure[3:4], ("gz", "gy"), up_d)
    hi = lax.ppermute(pressure[0:1], ("gz", "gy"), down_d)
    plate_2 = plate_last(scal, plate_now, plate_ext, pressure, motion, lo, hi, n_rows)
    air_2 = add_force(scal, air_2, came, press_now)
    return (air_2, plate_2)


def solution(mesh):
    in_specs = (
        P("gz", "gy", None),
        P("gz", "gy", None),
        P(("gz", "gy"), None),
        P(("gz", "gy"), None),
        P(),
        P(),
    )
    out_specs = (P("gz", "gy", None), P(("gz", "gy"), None))
    return jax.shard_map(shards, mesh=mesh, in_specs=in_specs, out_specs=out_specs, check_vma=False)
```

```python
import functools

import jax
import jax.numpy as jnp
from jax import lax
from jax.experimental import pallas as pl
from jax.experimental.pallas import tpu as pltpu
from jax.sharding import PartitionSpec as P

F32 = jnp.float32
C_PRESS = 0.5 / 1.01
HIGH = lax.Precision.HIGHEST


def params(mib):
    return pltpu.CompilerParams(vmem_limit_bytes=mib << 20)


class Place:
    def __init__(self, level, shift):
        self.level, self.shift = level, shift

    def __getitem__(self, i):
        if i == 0:
            return self.level[0]
        if i == 1:
            return self.shift[0]
        slab, strip = lax.axis_index("gz"), lax.axis_index("gy")
        return {2: slab * 8, 3: slab * lax.axis_size("gy") + strip, 4: strip, 5: slab}[i]


def placed(kernel):
    def run(level, shift, *refs):
        kernel(Place(level, shift), *refs)

    return run


def cost(nbytes):
    return pl.CostEstimate(flops=nbytes, bytes_accessed=nbytes, transcendentals=0)


def iota(shape, axis):
    return lax.broadcasted_iota(jnp.int32, shape, axis)


def left_right(x):
    width = x.shape[1]
    col = iota(x.shape, 1)
    west = jnp.where(col == 0, 0.0, pltpu.roll(x, 1, 1))
    east = jnp.where(col == width - 1, 0.0, pltpu.roll(x, width - 1, 1))
    return west + east


def up_down(x, above, below):
    height = x.shape[0]
    row = iota(x.shape, 0)
    up = jnp.where(row == 0, above, pltpu.roll(x, 1, 0))
    down = jnp.where(row == height - 1, below, pltpu.roll(x, height - 1, 0))
    return up + down


def sweep(load, count, above, below, emit):
    here = load(0)
    shape = here.shape
    width = shape[1]
    row, col = iota(shape, 0), iota(shape, 1)
    top, bottom, left, right = row == 0, row == 7, col == 0, col == width - 1
    from_above = above
    up, down = pltpu.roll(here, 1, 0), pltpu.roll(here, 7, 0)
    for i in range(count):
        if i + 1 < count:
            later = load(i + 1)
            later_up, later_down = pltpu.roll(later, 1, 0), pltpu.roll(later, 7, 0)
            from_below = later_down
        else:
            from_below = below
        west = jnp.where(left, 0.0, pltpu.roll(here, 1, 1))
        east = jnp.where(right, 0.0, pltpu.roll(here, width - 1, 1))
        vertical = jnp.where(top, from_above, up) + jnp.where(bottom, from_below, down)
        emit(i, here, west + east + vertical)
        if i + 1 < count:
            from_above = up
            here, up, down = later, later_up, later_down


def pack_kernel(now0, now1, old0, old1, plate_now, plate_prev, first, last):
    rows = plate_now.shape[0]
    cols = plate_now.shape[1]
    width = now0.shape[2]
    for out, now, old, edge, inner, r in (
        (first, now0, old0, 0, 1, 0),
        (last, now1, old1, 7, 6, rows - 4),
    ):
        here = now[:, edge, :]
        depth = here.shape[0]
        out[0:4, 0:cols] = plate_now[r : r + 4, :]
        out[4:8, 0:cols] = plate_prev[r : r + 4, :]
        out[:, cols : cols + width] = here
        around = left_right(here) + up_down(here, 0.0, 0.0) + now[:, inner, :]
        out[:, cols + width : cols + 2 * width] = 0.2 * here - old[:, edge, :] + 0.3 * around


def face_kernel(scal, here, inner, old, lo, hi, motion, on_chip, off_chip):
    height, width = here.shape[1], here.shape[2]
    strip = scal[4]
    lower_core = (scal[5] & 1) == 0

    def one(level, out):
        above = jnp.where(strip > 0, lo[pl.ds(level, 1), :], 0.0)
        below = jnp.where(strip < 7, hi[pl.ds(level, 1), :], 0.0)

        def emit(i, x, around):
            at = slice(8 * i, 8 * i + 8)
            out[at, :] = x
            part = 0.2 * x - old[0, at, :] + 0.3 * (around + inner[0, at, :])
            out[height + 8 * i : height + 8 * i + 8, :] = part

        sweep(lambda i: here[0, 8 * i : 8 * i + 8, :], height // 8, above, below, emit)
        row = iota((8, width), 0)
        ends = jnp.where(row == 0, above, jnp.where(row == 1, below, 0.0))
        out[2 * height : 2 * height + 8, :] = ends
        out[2 * height + 8 : 2 * height + 16, :] = motion[...]

    @pl.when(pl.program_id(0) == 0)
    def _():
        one(jnp.where(lower_core, 7, 0), on_chip)

    @pl.when(pl.program_id(0) == 1)
    def _():
        one(jnp.where(lower_core, 0, 7), off_chip)


def faces(scal, air_now, air_prev, lo, hi, motion, cols):
    depth, height, width = air_now.shape

    def plane(inner):
        def where(i, *scal):
            top = ((Place(*scal)[5] + i) & 1) == 0
            return (jnp.where(top, depth - 1 - inner, inner), 0, 0)

        return pl.BlockSpec((1, height, width), where)

    edge = pl.BlockSpec((8, width), lambda i, *scal: (0, cols // width))
    out = pl.BlockSpec((2 * height + 16, width), lambda i, *scal: (0, 0))
    return pl.pallas_call(
        placed(face_kernel),
        grid_spec=pltpu.PrefetchScalarGridSpec(
            num_scalar_prefetch=2,
            grid=(2,),
            in_specs=[
                plane(0),
                plane(1),
                plane(0),
                edge,
                edge,
                pl.BlockSpec((8, width), lambda i, *scal: (0, 0)),
            ],
            out_specs=[out, out],
        ),
        out_shape=[jax.ShapeDtypeStruct((2 * height + 16, width), F32)] * 2,
        compiler_params=params(59),
        cost_estimate=cost(5 << 20),
    )(*scal, air_now, air_now, air_prev, lo, hi, motion)


def air_kernel(scal, now, prev, on_chip, off_chip, ylo, yhi, out, press, keep, mid):
    level, shift, first, strip, slab = scal[0], scal[1], scal[2], scal[4], scal[5]
    t = pl.program_id(0)
    _, height, width = now.shape
    depth = 8
    strips = [slice(8 * i, 8 * i + 8) for i in range(height // 8)]
    y_lo = jnp.where(strip > 0, 1.0, 0.0).astype(F32)
    y_hi = jnp.where(strip < 7, 1.0, 0.0).astype(F32)
    lower_core = (slab & 1) == 0

    def zlo(first, count):
        at = slice(first, first + count)
        return jnp.where(lower_core, off_chip[at, :], on_chip[at, :])

    def zhi(first, count):
        at = slice(first, first + count)
        return jnp.where(lower_core, on_chip[at, :], off_chip[at, :])

    @pl.when(t == 0)
    def _():
        inside = jnp.where(slab > 0, 1.0, 0.0).astype(F32)
        for i, at in enumerate(strips):
            keep[0, at, :] = zlo(8 * i, 8)
            keep[depth + 1, at, :] = zhi(8 * i, 8)
            mid[0, at, :] = inside * (zlo(height + 8 * i, 8) + 0.3 * now[0, at, :])

    @pl.when(t == depth - 1)
    def _():
        inside = jnp.where(slab < 15, 1.0, 0.0).astype(F32)
        for i, at in enumerate(strips):
            mid[depth + 1, at, :] = inside * (zhi(height + 8 * i, 8) + 0.3 * now[0, at, :])

    @pl.when(t < depth)
    def _():
        for at in strips:
            keep[t + 1, at, :] = now[0, at, :]

    @pl.when((t >= 1) & (t <= depth))
    def _():
        z = t - 1
        above = y_lo * ylo[pl.ds(z, 1), 0:width]
        below = y_hi * yhi[pl.ds(z, 1), 0:width]

        def emit(i, x, around):
            at = strips[i]
            total = around + keep[z, at, :] + keep[z + 2, at, :]
            mid[z + 1, at, :] = 0.2 * x - prev[0, at, :] + 0.3 * total

        sweep(lambda i: keep[z + 1, strips[i], :], len(strips), above, below, emit)

    @pl.when(t >= 2)
    def _():
        z = t - 2
        at_bottom = jnp.where(z == 0, 0.3, 0.0).astype(F32)
        at_top = jnp.where(z == depth - 1, 0.3, 0.0).astype(F32)

        def rim(rows, line, r):
            row = rows[pl.ds(z, 1), width : 2 * width] + 0.3 * line
            return row + at_bottom * zlo(r, 1) + at_top * zhi(r, 1)

        above = y_lo * rim(ylo, keep[z + 1, 0:1, :], 2 * height)
        below = y_hi * rim(yhi, keep[z + 1, height - 1 : height, :], 2 * height + 1)

        def emit(i, x, around):
            at = strips[i]
            total = around + mid[z, at, :] + mid[z + 2, at, :]
            out[0, at, :] = 0.2 * x - keep[z + 1, at, :] + 0.3 * total

        sweep(lambda i: mid[z + 1, strips[i], :], len(strips), above, below, emit)

    @pl.when(t == depth)
    def _():
        upper = jnp.clip(level + 1 - first, -1, depth) + 1
        lower = jnp.clip(level - first, -1, depth) + 1
        for i, at in enumerate(strips):
            y = iota((8, width), 0) + (strip * height + 8 * i - shift)
            gap = keep[upper, at, :] - keep[lower, at, :]
            press[at, :] = jnp.where((y >= 0) & (y < 512), (0.5 * C_PRESS) * gap, 0.0)


def air_steps(scal, now, prev, on_chip, off_chip, ylo, yhi, cols):
    depth, height, width = now.shape

    def plane(lag):
        return pl.BlockSpec(
            (1, height, width), lambda t, *scal: (jnp.clip(t - lag, 0, depth - 1), 0, 0)
        )

    z_face = pl.BlockSpec((2 * height + 16, width), lambda t, *scal: (0, 0))
    rows = pl.BlockSpec((8, 2 * width), lambda t, *scal: (0, cols // (2 * width)))
    return pl.pallas_call(
        placed(air_kernel),
        grid_spec=pltpu.PrefetchScalarGridSpec(
            num_scalar_prefetch=2,
            grid=(depth + 2,),
            in_specs=[plane(0), plane(1), z_face, z_face, rows, rows],
            out_specs=[
                plane(2),
                pl.BlockSpec((height, width), lambda t, *scal: (0, 0)),
            ],
            scratch_shapes=[pltpu.VMEM((depth + 2, height, width), F32)] * 2,
        ),
        out_shape=[
            jax.ShapeDtypeStruct(now.shape, F32),
            jax.ShapeDtypeStruct((height, width), F32),
        ],
        compiler_params=params(59),
        cost_estimate=cost(24 << 20),
    )(*scal, now, prev, on_chip, off_chip, ylo, yhi)


def fold_row(row):
    return jnp.concatenate([row[:, 128 * q : 128 * q + 128] for q in range(8)], axis=0)


def press_kernel(scal, up2, up1, at0, dn1, pup1, pat0, out):
    level, shift, base = scal[0], scal[1], scal[2]
    depth = 8
    width = up1.shape[2]

    def mine(z):
        return jnp.where((z >= base) & (z < base + depth), 1.0, 0.0).astype(F32)

    here = (level + 2 >= base) & (level - 1 < base + depth)

    @pl.when(jnp.logical_not(here))
    def _():
        out[...] = jnp.zeros(out.shape, F32)

    @pl.when(here)
    def _():
        m1, m0 = mine(level + 1), mine(level)
        m2, mm = mine(level + 2), mine(level - 1)
        b = shift & 31
        turn = (32 - b) & 31
        for k in range(up1.shape[1] // 32):
            at = slice(32 * k, 32 * k + 32)
            press = m1 * up1[0, at, :] - m0 * at0[0, at, :]
            vertical = m2 * up2[0, at, :] - 3.0 * press - mm * dn1[0, at, :]
            older = m1 * pup1[0, at, :] - m0 * pat0[0, at, :]
            r0 = pltpu.roll(press, turn, 0)
            r1 = pltpu.roll(0.3 * vertical - older, turn, 0)
            folded = [fold_row(r0[i : i + 1]) for i in range(32) if i & 3 in (0, 3)]
            for y in range(8):
                tile = slice(8 * k, 8 * k + 8)
                out[y, 8 * k : 8 * k + 4, 0:width] = r0[4 * y : 4 * y + 4]
                out[y, 8 * k + 4 : 8 * k + 8, 0:width] = r1[4 * y : 4 * y + 4]
                out[y, tile, width : width + 128] = folded[(2 * y - 1) % 16]
                out[y, tile, width + 128 : width + 256] = folded[(2 * y + 2) % 16]


def front_kernel(scal, *refs):
    pack_kernel(*refs[0:6], *refs[12:14])
    press_kernel(scal, *refs[6:12], refs[14])


def front(scal, air_now, air_prev, plate_now, plate_prev):
    depth, height, width = air_now.shape
    rows, cols = plate_now.shape
    low = pl.BlockSpec((depth, 8, width), lambda i, *scal: (0, 0, 0))
    high = pl.BlockSpec((depth, 8, width), lambda i, *scal: (0, height // 8 - 1, 0))
    plate = pl.BlockSpec((rows, cols), lambda i, *scal: (0, 0))
    pack = pl.BlockSpec((8, cols + 2 * width), lambda i, *scal: (0, 0))

    def plane(offset):
        def where(k, *scal):
            scal = Place(*scal)
            return (jnp.clip(scal[0] + offset - scal[2], 0, depth - 1), 0, 0)

        return pl.BlockSpec((1, height, width), where)

    return pl.pallas_call(
        placed(front_kernel),
        grid_spec=pltpu.PrefetchScalarGridSpec(
            num_scalar_prefetch=2,
            grid=(1,),
            in_specs=[low, high, low, high, plate, plate]
            + [plane(2), plane(1), plane(0), plane(-1), plane(1), plane(0)],
            out_specs=[pack, pack, pl.BlockSpec((8, 32, width + 256), lambda k, *scal: (0, 0, 0))],
        ),
        out_shape=[jax.ShapeDtypeStruct((8, cols + 2 * width), F32)] * 2
        + [jax.ShapeDtypeStruct((8, 32, width + 256), F32)],
        compiler_params=params(59),
        cost_estimate=cost(6 << 20),
    )(
        *scal,
        *(air_now, air_now, air_prev, air_prev, plate_now, plate_prev),
        *(air_now, air_now, air_now, air_now, air_prev, air_prev),
    )


def flat_laplace(x):
    height = x.shape[0]
    return left_right(x) + pltpu.roll(x, 1, 0) + pltpu.roll(x, height - 1, 0) - 4.0 * x


def inside_rows(shape, first, last_row):
    row = iota(shape, 0) + first
    return (row >= 0) & (row < last_row)


def plate_kernel(n_rows, scal, now, prev, lo, hi, next_ext, motion):
    rows, cols = now.shape
    first = scal[3] * rows - 4
    here = now[...]
    ext = jnp.concatenate([lo[0:4, 0:cols], here, hi[0:4, 0:cols]], axis=0)
    old = jnp.concatenate([lo[4:8, 0:cols], prev[...], hi[4:8, 0:cols]], axis=0)
    ok = inside_rows(ext.shape, first, n_rows)
    inner = jnp.where(ok, flat_laplace(ext), 0.0)
    bend = flat_laplace(inner)
    nxt = (2.0 * ext - 0.99 * old - 0.04 * bend) * (1.0 / 1.01)
    nxt = jnp.where(ok, nxt, 0.0)
    next_ext[...] = nxt
    both = jnp.concatenate([here - prev[...], nxt[4 : 4 + rows] - here], axis=0)
    fold = jnp.where((iota((512, 128), 0) >> 2) == iota((512, 128), 1), 1.0, 0.0)
    parts = [
        jnp.dot(both[:, 512 * q : 512 * q + 512], fold, precision=HIGH, preferred_element_type=F32)
        for q in range(cols // 512)
    ]
    narrow = jnp.concatenate(parts, axis=1)
    pick = jnp.where(iota((8, 32), 0) == (iota((8, 32), 1) >> 2), 1.0 / 16.0, 0.0)
    motion[...] = jnp.dot(pick, narrow, precision=HIGH, preferred_element_type=F32)


def plate_first(scal, now, prev, lo, hi, n_rows):
    rows, cols = now.shape
    return pl.pallas_call(
        placed(functools.partial(plate_kernel, n_rows)),
        in_specs=[pl.BlockSpec(memory_space=pltpu.SMEM)] * 2
        + [pl.BlockSpec(memory_space=pltpu.VMEM)] * 4,
        out_specs=[pl.BlockSpec(memory_space=pltpu.VMEM)] * 2,
        out_shape=[
            jax.ShapeDtypeStruct((rows + 8, cols), F32),
            jax.ShapeDtypeStruct((8, cols // 4), F32),
        ],
        compiler_params=params(16),
        cost_estimate=cost(4 << 20),
    )(*scal, now, prev, lo, hi)


def carries(shape, strip, b):
    return (4 * strip + (iota(shape, 0) & 3) + b) >= 32


def to_plate_kernel(scal, came, motion, out):
    shift, strip = scal[1], scal[4]
    a, b = shift >> 5, shift & 31
    move = motion[...]
    width = move.shape[1]
    carry = carries(move.shape, strip, b)
    before = (4 * strip - 1 + b) >> 5
    behind = (4 * strip + 4 + b) >> 5

    def folded(block, lane):
        ok = jnp.where((block >= 0) & (block < 32), 1.0, 0.0).astype(F32)
        at = pl.multiple_of(8 * jnp.clip(block, 0, 31), 8)
        return came[pl.ds(at, 8), lane : lane + 128] * ok

    slab = scal[5]
    pair = jnp.clip((scal[0] - 1) >> 3, 0, 14)
    aside = (slab < pair) | (slab > pair + 1)
    for dest in range(16):
        at = pl.multiple_of(8 * (dest + a), 8)
        after = pl.multiple_of(8 * jnp.minimum(dest + a + 1, 31), 8)
        tile = jnp.where(carry, came[pl.ds(after, 8), 0:width], came[pl.ds(at, 8), 0:width])
        wants = aside & ((pair == dest) | (pair + 1 == dest))
        out[dest, :, 0:width] = jnp.where(wants, move, tile)
        out[dest, :, width : width + 128] = folded(dest + a + before, width)
        out[dest, :, width + 128 : width + 256] = folded(dest + a + behind, width + 128)


def to_plate(scal, came, motion):
    width = motion.shape[1]
    return pl.pallas_call(
        placed(to_plate_kernel),
        in_specs=[pl.BlockSpec(memory_space=pltpu.SMEM)] * 2
        + [pl.BlockSpec(memory_space=pltpu.VMEM)] * 2,
        out_specs=pl.BlockSpec(memory_space=pltpu.VMEM),
        out_shape=jax.ShapeDtypeStruct((16, 8, width + 256), F32),
        compiler_params=params(16),
        cost_estimate=cost(2 << 20),
    )(*scal, came, motion)


def to_air_kernel(scal, came, motion, on_chip, off_chip, pressure, out, moves):
    shift, strip, slab = scal[1], scal[4], scal[5]
    a, b = shift >> 5, shift & 31
    width = out.shape[2]
    pair = jnp.clip((scal[0] - 1) >> 3, 0, 14)
    pressure[...] = came[pair] + came[pair + 1]
    for src in range(16):
        moves[src] = came[src, :, 0:width]
    moves[slab] = motion[...]

    moves[slab ^ 1] = on_chip[...]

    @pl.when((slab > 0) & (slab < 15))
    def _():
        moves[jnp.where((slab & 1) == 0, slab - 1, slab + 1)] = off_chip[...]

    shape = (8, width)
    carry = carries(shape, strip, b)
    row = iota(shape, 0)
    place = (4 * strip + (row & 3) + b) & 31
    first_field = row < 4

    def tile(block):
        def one(src):
            ok = jnp.where((src >= 0) & (src < 16), 1.0, 0.0).astype(F32)
            return moves[jnp.clip(src, 0, 15)] * ok

        return jnp.where(carry, one(block - a - 1), one(block - a))

    for s in range(8):
        tiles = [tile(4 * s + k) for k in range(4)]
        for k in range(4):
            out[s, 8 * k : 8 * k + 8, :] = tiles[k]
        if s > 0:
            before = jnp.where(first_field & (place == 31), tile(4 * s - 1), 0.0)
        else:
            before = jnp.zeros(shape, F32)
        if s < 7:
            behind = jnp.where(first_field & (place == 0), tile(4 * s + 4), 0.0)
        else:
            behind = jnp.zeros(shape, F32)
        out[s, 32:40, :] = before + pltpu.roll(behind, 4, 0)


def to_air(scal, came, motion, on_chip, off_chip):
    width = motion.shape[1]
    return pl.pallas_call(
        placed(to_air_kernel),
        in_specs=[pl.BlockSpec(memory_space=pltpu.SMEM)] * 2
        + [pl.BlockSpec(memory_space=pltpu.VMEM)] * 4,
        out_specs=[pl.BlockSpec(memory_space=pltpu.VMEM)] * 2,
        out_shape=[
            jax.ShapeDtypeStruct((8, width + 256), F32),
            jax.ShapeDtypeStruct((8, 40, width), F32),
        ],
        scratch_shapes=[pltpu.VMEM((16, 8, width), F32)],
        compiler_params=params(16),
        cost_estimate=cost(2 << 20),
    )(*scal, came, motion, on_chip, off_chip)


def force_kernel(scal, field, came, press, out, q, r):
    level, shift, base = scal[0], scal[1], scal[2]
    t = pl.program_id(0)
    height, width = q.shape
    depth = 8
    b = shift & 31

    @pl.when(t == 0)
    def _():
        for k in range(height // 32):
            for f, ref in ((0, r), (1, q)):
                rows = [came[y, 8 * k + 4 * f : 8 * k + 4 * f + 4, :] for y in range(8)]
                ref[32 * k : 32 * k + 32, :] = pltpu.roll(jnp.concatenate(rows, axis=0), b, 0)
        rim = came[0, 32:40, :]
        for y in range(1, 8):
            rim = rim + came[y, 32:40, :]
        above = jnp.sum(rim[0:4], axis=0, keepdims=True)
        below = jnp.sum(rim[4:8], axis=0, keepdims=True)
        motion = r[...]
        around = left_right(motion) + up_down(motion, above, below)
        q[...] = (0.55 - 0.6) * motion + 0.15 * around + 0.5 * q[...] + press[...]

    z = jnp.clip(level - 1 + t - base, 0, depth - 1) + base

    def is_level(other):
        return jnp.where(z == other, 1.0, 0.0).astype(F32)

    wq = is_level(level) - is_level(level + 1)
    wr = 0.15 * (is_level(level - 1) - is_level(level + 2))
    out[0] = field[0] + wq * q[...] + wr * r[...]


def add_force(scal, field, came, press):
    depth, height, width = field.shape

    def where(t, *scal):
        scal = Place(*scal)
        return (jnp.clip(scal[0] - 1 + t - scal[2], 0, depth - 1), 0, 0)

    plane = pl.BlockSpec((1, height, width), where)
    return pl.pallas_call(
        placed(force_kernel),
        grid_spec=pltpu.PrefetchScalarGridSpec(
            num_scalar_prefetch=2,
            grid=(4,),
            in_specs=[
                plane,
                pl.BlockSpec((8, 40, width), lambda t, *scal: (0, 0, 0)),
                pl.BlockSpec((height, width), lambda t, *scal: (0, 0)),
            ],
            out_specs=plane,
            scratch_shapes=[pltpu.VMEM((height, width), F32)] * 2,
        ),
        out_shape=jax.ShapeDtypeStruct(field.shape, F32),
        input_output_aliases={2: 0},
        compiler_params=params(24),
        cost_estimate=cost(4 << 20),
    )(*scal, field, came, press)


def unfold(tile):
    return jnp.concatenate([tile[q : q + 1] for q in range(8)], axis=1)


def plate_last_kernel(n_rows, scal, now, next_ext, pressure, motion, out):
    rows, cols = now.shape
    first = scal[3] * rows - 4
    width = motion.shape[1]
    press = pressure[0:4, 0:width]
    lo = unfold(pressure[:, width : width + 128])
    hi = unfold(pressure[:, width + 128 : width + 256])
    around = left_right(press) + up_down(press, lo, hi) - 4.0 * press
    later = 2.0 * press + 0.3 * around + pressure[4:8, 0:width] - motion[0:4]
    lines = jnp.concatenate([press, later, lo, hi, jnp.zeros((6, width), F32)], axis=0)
    spread = jnp.where((iota((128, 512), 1) >> 2) == iota((128, 512), 0), 1.0, 0.0)
    parts = [
        jnp.dot(lines[:, 128 * q : 128 * q + 128], spread, precision=HIGH, preferred_element_type=F32)
        for q in range(width // 128)
    ]
    wide = jnp.concatenate(parts, axis=1)
    e = iota((24, 16), 0)
    line = iota((24, 16), 1)
    source = jnp.where(e < 4, 8, jnp.where(e >= 20, 9, (e - 4) >> 2))
    pick = jnp.where(line == source, C_PRESS, 0.0)
    push = jnp.dot(pick, wide, precision=HIGH, preferred_element_type=F32)
    pick = jnp.where(iota((16, 16), 1) == 4 + (iota((16, 16), 0) >> 2), C_PRESS, 0.0)
    push_last = jnp.dot(pick, wide, precision=HIGH, preferred_element_type=F32)
    ok = inside_rows(next_ext.shape, first, n_rows)
    mid = jnp.where(ok, next_ext[...] + push, 0.0)
    inner = jnp.where(ok, flat_laplace(mid), 0.0)
    bend = flat_laplace(inner)[4 : 4 + rows]
    final = (2.0 * mid[4 : 4 + rows] - 0.99 * now[...] - 0.04 * bend) * (1.0 / 1.01)
    out[...] = final + push_last


def plate_last(scal, now, next_ext, pressure, motion, n_rows):
    return pl.pallas_call(
        placed(functools.partial(plate_last_kernel, n_rows)),
        in_specs=[pl.BlockSpec(memory_space=pltpu.SMEM)] * 2
        + [pl.BlockSpec(memory_space=pltpu.VMEM)] * 4,
        out_specs=pl.BlockSpec(memory_space=pltpu.VMEM),
        out_shape=jax.ShapeDtypeStruct(now.shape, F32),
        compiler_params=params(16),
        cost_estimate=cost(4 << 20),
    )(*scal, now, next_ext, pressure, motion)


def neighbours(n):
    return [(i, i + 1) for i in range(n - 1)], [(i + 1, i) for i in range(n - 1)]


def shards(air_now, air_prev, plate_now, plate_prev, plate_level, plate_shift):
    depth, height, width = air_now.shape
    n_gz, n_gy = lax.axis_size("gz"), lax.axis_size("gy")
    n_rows = plate_now.shape[0] * n_gz * n_gy
    cols = plate_now.shape[1]
    scal = (plate_level, plate_shift)
    up_d, down_d = neighbours(n_gz * n_gy)

    first, last, sent = front(scal, air_now, air_prev, plate_now, plate_prev)
    lo = lax.ppermute(last, ("gz", "gy"), up_d)
    hi = lax.ppermute(first, ("gz", "gy"), down_d)
    sent, lo, hi = lax.optimization_barrier((sent, lo, hi))
    came = lax.all_to_all(sent, "gy", 0, 0).reshape(256, width + 256)

    plate_ext, motion = plate_first(scal, plate_now, plate_prev, lo, hi, n_rows)
    on_chip, off_chip = faces(scal, air_now, air_prev, lo, hi, motion, cols)
    on_chip = lax.ppermute(on_chip, "gz", [(i, i ^ 1) for i in range(n_gz)])
    across = [(i, i + 1) for i in range(1, n_gz - 1, 2)]
    off_chip = lax.ppermute(off_chip, "gz", across + [(j, i) for i, j in across])

    came = lax.all_to_all(to_plate(scal, came, motion), "gz", 0, 0)
    air_2, press_now = air_steps(scal, air_now, air_prev, on_chip, off_chip, lo, hi, cols)
    end = 2 * height + 8
    pressure, sent = to_air(scal, came, motion, on_chip[end : end + 8], off_chip[end : end + 8])
    came = lax.all_to_all(sent, "gy", 0, 0)

    plate_2 = plate_last(scal, plate_now, plate_ext, pressure, motion, n_rows)
    air_2 = add_force(scal, air_2, came, press_now)
    return (air_2, plate_2)


def solution(mesh):
    in_specs = (
        P("gz", "gy", None),
        P("gz", "gy", None),
        P(("gz", "gy"), None),
        P(("gz", "gy"), None),
        P(),
        P(),
    )
    out_specs = (P("gz", "gy", None), P(("gz", "gy"), None))
    return jax.shard_map(shards, mesh=mesh, in_specs=in_specs, out_specs=out_specs, check_vma=False)
```

```python
import functools

import jax
import jax.numpy as jnp
from jax import lax
from jax.experimental import pallas as pl
from jax.experimental.pallas import tpu as pltpu
from jax.sharding import PartitionSpec as P

F32 = jnp.float32
C_PRESS = 0.5 / 1.01
HIGH = lax.Precision.HIGHEST


def params(mib):
    return pltpu.CompilerParams(vmem_limit_bytes=mib << 20)


class Place:
    def __init__(self, level, shift):
        self.level, self.shift = level, shift

    def __getitem__(self, i):
        if i == 0:
            return self.level[0]
        if i == 1:
            return self.shift[0]
        slab, strip = lax.axis_index("gz"), lax.axis_index("gy")
        return {2: slab * 8, 3: slab * lax.axis_size("gy") + strip, 4: strip, 5: slab}[i]


def placed(kernel):
    def run(level, shift, *refs):
        kernel(Place(level, shift), *refs)

    return run


def cost(nbytes):
    return pl.CostEstimate(flops=nbytes, bytes_accessed=nbytes, transcendentals=0)


def iota(shape, axis):
    return lax.broadcasted_iota(jnp.int32, shape, axis)


def left_right(x):
    width = x.shape[1]
    col = iota(x.shape, 1)
    west = jnp.where(col == 0, 0.0, pltpu.roll(x, 1, 1))
    east = jnp.where(col == width - 1, 0.0, pltpu.roll(x, width - 1, 1))
    return west + east


def up_down(x, above, below):
    height = x.shape[0]
    row = iota(x.shape, 0)
    up = jnp.where(row == 0, above, pltpu.roll(x, 1, 0))
    down = jnp.where(row == height - 1, below, pltpu.roll(x, height - 1, 0))
    return up + down


def sweep(load, count, above, below, emit):
    here = load(0)
    shape = here.shape
    width = shape[1]
    row, col = iota(shape, 0), iota(shape, 1)
    top, bottom, left, right = row == 0, row == 7, col == 0, col == width - 1
    from_above = above
    up, down = pltpu.roll(here, 1, 0), pltpu.roll(here, 7, 0)
    for i in range(count):
        if i + 1 < count:
            later = load(i + 1)
            later_up, later_down = pltpu.roll(later, 1, 0), pltpu.roll(later, 7, 0)
            from_below = later_down
        else:
            from_below = below
        west = jnp.where(left, 0.0, pltpu.roll(here, 1, 1))
        east = jnp.where(right, 0.0, pltpu.roll(here, width - 1, 1))
        vertical = jnp.where(top, from_above, up) + jnp.where(bottom, from_below, down)
        emit(i, here, west + east + vertical)
        if i + 1 < count:
            from_above = up
            here, up, down = later, later_up, later_down


def pack_kernel(now0, now1, old0, old1, plate_now, plate_prev, first, last):
    rows = plate_now.shape[0]
    cols = plate_now.shape[1]
    width = now0.shape[2]
    for out, now, old, edge, inner, r in (
        (first, now0, old0, 0, 1, 0),
        (last, now1, old1, 7, 6, rows - 4),
    ):
        here = now[:, edge, :]
        depth = here.shape[0]
        out[0:4, 0:cols] = plate_now[r : r + 4, :]
        out[4:8, 0:cols] = plate_prev[r : r + 4, :]
        out[:, cols : cols + width] = here
        around = left_right(here) + up_down(here, 0.0, 0.0) + now[:, inner, :]
        out[:, cols + width : cols + 2 * width] = 0.2 * here - old[:, edge, :] + 0.3 * around


def face_kernel(scal, here, inner, old, on_chip, off_chip):
    height = here.shape[1]

    def one(out):
        def emit(i, x, around):
            at = slice(8 * i, 8 * i + 8)
            out[at, :] = x
            part = 0.2 * x - old[0, at, :] + 0.3 * (around + inner[0, at, :])
            out[height + 8 * i : height + 8 * i + 8, :] = part

        sweep(lambda i: here[0, 8 * i : 8 * i + 8, :], height // 8, 0.0, 0.0, emit)

    @pl.when(pl.program_id(0) == 0)
    def _():
        one(on_chip)

    @pl.when(pl.program_id(0) == 1)
    def _():
        one(off_chip)


def faces(scal, air_now, air_prev):
    depth, height, width = air_now.shape

    def plane(inner):
        def where(i, *scal):
            top = ((Place(*scal)[5] + i) & 1) == 0
            return (jnp.where(top, depth - 1 - inner, inner), 0, 0)

        return pl.BlockSpec((1, height, width), where)

    out = pl.BlockSpec((2 * height, width), lambda i, *scal: (0, 0))
    return pl.pallas_call(
        placed(face_kernel),
        grid_spec=pltpu.PrefetchScalarGridSpec(
            num_scalar_prefetch=2,
            grid=(2,),
            in_specs=[
                plane(0),
                plane(1),
                plane(0),
            ],
            out_specs=[out, out],
        ),
        out_shape=[jax.ShapeDtypeStruct((2 * height, width), F32)] * 2,
        compiler_params=params(59),
        cost_estimate=cost(5 << 20),
    )(*scal, air_now, air_now, air_prev)


def corner_kernel(scal, lo, hi, on_chip, off_chip):
    strip = scal[4]
    lower_core = (scal[5] & 1) == 0
    row = iota(on_chip.shape, 0)

    def ends(level):
        above = jnp.where(strip > 0, lo[level : level + 1, :], 0.0)
        below = jnp.where(strip < 7, hi[level : level + 1, :], 0.0)
        return jnp.where(row == 0, above, jnp.where(row == 1, below, 0.0))

    bottom, top = ends(0), ends(7)
    on_chip[...] = jnp.where(lower_core, top, bottom)
    off_chip[...] = jnp.where(lower_core, bottom, top)


def corners(scal, lo, hi, cols, width):
    edge = pl.BlockSpec((8, width), lambda i, *scal: (0, cols // width))
    out = pl.BlockSpec((8, width), lambda i, *scal: (0, 0))
    return pl.pallas_call(
        placed(corner_kernel),
        grid_spec=pltpu.PrefetchScalarGridSpec(
            num_scalar_prefetch=2, grid=(1,), in_specs=[edge, edge], out_specs=[out, out]
        ),
        out_shape=[jax.ShapeDtypeStruct((8, width), F32)] * 2,
        compiler_params=params(16),
        cost_estimate=cost(1 << 20),
    )(*scal, lo, hi)


def air_kernel(
    scal, now, prev, on_chip, off_chip, ylo, yhi,
    out, press, keep, mid, older, sems,
):
    level, shift, first, strip, slab = scal[0], scal[1], scal[2], scal[4], scal[5]
    t = pl.program_id(0)
    depth, height, width = now.shape
    strips = [slice(8 * i, 8 * i + 8) for i in range(height // 8)]
    y_lo = jnp.where(strip > 0, 1.0, 0.0).astype(F32)
    y_hi = jnp.where(strip < 7, 1.0, 0.0).astype(F32)
    lower_core = (slab & 1) == 0

    def zlo(first, count):
        at = slice(first, first + count)
        return jnp.where(lower_core, off_chip[at, :], on_chip[at, :])

    def zhi(first, count):
        at = slice(first, first + count)
        return jnp.where(lower_core, on_chip[at, :], off_chip[at, :])

    def fetch_now(z):
        return pltpu.make_async_copy(now.at[z], keep.at[z + 1], sems.at[0, z])

    def fetch_prev(z):
        return pltpu.make_async_copy(prev.at[z], older.at[z], sems.at[1, z])

    @pl.when(t == 0)
    def _():
        for z in range(depth):
            fetch_now(z).start()
            fetch_prev(z).start()

    @pl.when(t < depth)
    def _():
        fetch_now(t).wait()

    @pl.when((t >= 1) & (t <= depth))
    def _():
        fetch_prev(t - 1).wait()

    def outer(target, source, level, inside):
        inside = jnp.where(inside, 1.0, 0.0).astype(F32)
        for i, at in enumerate(strips):
            mid[target, at, :] = inside * (source(height + 8 * i, 8) + 0.3 * keep[level, at, :])

    @pl.when(t == 0)
    def _():
        for i, at in enumerate(strips):
            keep[0, at, :] = zlo(8 * i, 8)
            keep[depth + 1, at, :] = zhi(8 * i, 8)
        outer(0, zlo, 1, slab > 0)

    @pl.when(t == depth - 1)
    def _():
        outer(depth + 1, zhi, depth, slab < 15)

    @pl.when((t >= 1) & (t <= depth))
    def _():
        z = t - 1
        above = y_lo * ylo[pl.ds(z, 1), 0:width]
        below = y_hi * yhi[pl.ds(z, 1), 0:width]

        def emit(i, x, around):
            at = strips[i]
            total = around + keep[z, at, :] + keep[z + 2, at, :]
            mid[z + 1, at, :] = 0.2 * x - older[z, at, :] + 0.3 * total

        sweep(lambda i: keep[z + 1, strips[i], :], len(strips), above, below, emit)

    @pl.when(t >= 2)
    def _():
        z = t - 2

        def rim(rows, line):
            return rows[pl.ds(z, 1), width : 2 * width] + 0.3 * line

        above = y_lo * rim(ylo, keep[z + 1, 0:1, :])
        below = y_hi * rim(yhi, keep[z + 1, height - 1 : height, :])

        def emit(i, x, around):
            at = strips[i]
            total = around + mid[z, at, :] + mid[z + 2, at, :]
            out[0, at, :] = 0.2 * x - keep[z + 1, at, :] + 0.3 * total

        sweep(lambda i: mid[z + 1, strips[i], :], len(strips), above, below, emit)

    @pl.when(t == depth)
    def _():
        upper = jnp.clip(level + 1 - first, -1, depth) + 1
        lower = jnp.clip(level - first, -1, depth) + 1
        for i, at in enumerate(strips):
            y = iota((8, width), 0) + (strip * height + 8 * i - shift)
            gap = keep[upper, at, :] - keep[lower, at, :]
            press[at, :] = jnp.where((y >= 0) & (y < 512), (0.5 * C_PRESS) * gap, 0.0)


def air_steps(scal, now, prev, on_chip, off_chip, ylo, yhi, cols):
    depth, height, width = now.shape

    def plane(lag):
        return pl.BlockSpec(
            (1, height, width), lambda t, *scal: (jnp.clip(t - lag, 0, depth - 1), 0, 0)
        )

    whole = pl.BlockSpec(memory_space=pl.ANY)

    z_face = pl.BlockSpec((2 * height, width), lambda t, *scal: (0, 0))
    rows = pl.BlockSpec((8, 2 * width), lambda t, *scal: (0, cols // (2 * width)))
    return pl.pallas_call(
        placed(air_kernel),
        grid_spec=pltpu.PrefetchScalarGridSpec(
            num_scalar_prefetch=2,
            grid=(depth + 2,),
            in_specs=[whole, whole, z_face, z_face, rows, rows],
            out_specs=[
                plane(2),
                pl.BlockSpec((height, width), lambda t, *scal: (0, 0)),
            ],
            scratch_shapes=[pltpu.VMEM((depth + 2, height, width), F32)] * 2
            + [pltpu.VMEM(now.shape, F32), pltpu.SemaphoreType.DMA((2, depth))],
        ),
        out_shape=[
            jax.ShapeDtypeStruct(now.shape, F32),
            jax.ShapeDtypeStruct((height, width), F32),
        ],
        compiler_params=params(59),
        cost_estimate=cost(24 << 20),
    )(*scal, now, prev, on_chip, off_chip, ylo, yhi)


def fold_row(row):
    return jnp.concatenate([row[:, 128 * q : 128 * q + 128] for q in range(8)], axis=0)


def unfold(tile):
    return jnp.concatenate([tile[q : q + 1] for q in range(8)], axis=1)


def press_kernel(scal, up2, up1, at0, dn1, pup1, pat0, out):
    level, shift, base = scal[0], scal[1], scal[2]
    depth = 8
    width = up1.shape[2]

    def mine(z):
        return jnp.where((z >= base) & (z < base + depth), 1.0, 0.0).astype(F32)

    here = (level + 2 >= base) & (level - 1 < base + depth)

    @pl.when(jnp.logical_not(here))
    def _():
        out[...] = jnp.zeros(out.shape, F32)

    @pl.when(here)
    def _():
        m1, m0 = mine(level + 1), mine(level)
        m2, mm = mine(level + 2), mine(level - 1)
        b = shift & 31
        turn = (32 - b) & 31
        for k in range(up1.shape[1] // 32):
            at = slice(32 * k, 32 * k + 32)
            press = m1 * up1[0, at, :] - m0 * at0[0, at, :]
            vertical = m2 * up2[0, at, :] - 3.0 * press - mm * dn1[0, at, :]
            older = m1 * pup1[0, at, :] - m0 * pat0[0, at, :]
            r0 = pltpu.roll(press, turn, 0)
            r1 = pltpu.roll(0.3 * vertical - older, turn, 0)
            folded = [fold_row(r0[i : i + 1]) for i in range(32) if i & 3 in (0, 3)]
            for y in range(8):
                tile = slice(8 * k, 8 * k + 8)
                out[y, 8 * k : 8 * k + 4, 0:width] = r0[4 * y : 4 * y + 4]
                out[y, 8 * k + 4 : 8 * k + 8, 0:width] = r1[4 * y : 4 * y + 4]
                out[y, tile, width : width + 128] = folded[(2 * y - 1) % 16]
                out[y, tile, width + 128 : width + 256] = folded[(2 * y + 2) % 16]


def front_kernel(scal, *refs):
    pack_kernel(*refs[0:6], *refs[12:14])
    press_kernel(scal, *refs[6:12], refs[14])


def front(scal, air_now, air_prev, plate_now, plate_prev):
    depth, height, width = air_now.shape
    rows, cols = plate_now.shape
    low = pl.BlockSpec((depth, 8, width), lambda i, *scal: (0, 0, 0))
    high = pl.BlockSpec((depth, 8, width), lambda i, *scal: (0, height // 8 - 1, 0))
    plate = pl.BlockSpec((rows, cols), lambda i, *scal: (0, 0))
    pack = pl.BlockSpec((8, cols + 2 * width), lambda i, *scal: (0, 0))

    def plane(offset):
        def where(k, *scal):
            scal = Place(*scal)
            return (jnp.clip(scal[0] + offset - scal[2], 0, depth - 1), 0, 0)

        return pl.BlockSpec((1, height, width), where)

    return pl.pallas_call(
        placed(front_kernel),
        grid_spec=pltpu.PrefetchScalarGridSpec(
            num_scalar_prefetch=2,
            grid=(1,),
            in_specs=[low, high, low, high, plate, plate]
            + [plane(2), plane(1), plane(0), plane(-1), plane(1), plane(0)],
            out_specs=[pack, pack]
            + [pl.BlockSpec((8, 32, width + 256), lambda k, *scal: (0, 0, 0))],
        ),
        out_shape=[jax.ShapeDtypeStruct((8, cols + 2 * width), F32)] * 2
        + [jax.ShapeDtypeStruct((8, 32, width + 256), F32)],
        compiler_params=params(59),
        cost_estimate=cost(6 << 20),
    )(
        *scal,
        *(air_now, air_now, air_prev, air_prev, plate_now, plate_prev),
        *(air_now, air_now, air_now, air_now, air_prev, air_prev),
    )


def flat_laplace(x):
    height = x.shape[0]
    return left_right(x) + pltpu.roll(x, 1, 0) + pltpu.roll(x, height - 1, 0) - 4.0 * x


def inside_rows(shape, first, last_row):
    row = iota(shape, 0) + first
    return (row >= 0) & (row < last_row)


def plate_step(ext, old, ok):
    inner = jnp.where(ok, flat_laplace(ext), 0.0)
    bend = flat_laplace(inner)
    return (2.0 * ext - 0.99 * old - 0.04 * bend) * (1.0 / 1.01)


def plate_kernel(n_rows, scal, now, prev, motion):
    rows, cols = now.shape
    first = scal[3] * rows - 4
    here = now[...]
    far = jnp.zeros((4, cols), F32)
    ext = jnp.concatenate([far, here, far], axis=0)
    old = jnp.concatenate([far, prev[...], far], axis=0)
    ok = inside_rows(ext.shape, first, n_rows)
    nxt = jnp.where(ok, plate_step(ext, old, ok), 0.0) - ext
    both = jnp.concatenate([here - prev[...], nxt], axis=0)
    fold = jnp.where((iota((512, 128), 0) >> 2) == iota((512, 128), 1), 1.0, 0.0)
    parts = [
        jnp.dot(both[:, 512 * q : 512 * q + 512], fold, precision=HIGH, preferred_element_type=F32)
        for q in range(cols // 512)
    ]
    narrow = jnp.concatenate(parts, axis=1)
    width = narrow.shape[1]
    row = iota((16, 40), 0)
    source = jnp.where(row < 4, row, jnp.where(row < 8, row + 1, jnp.where(row == 8, 4, 9)))
    pick = jnp.where((source == (iota((16, 40), 1) >> 2)) & (row < 10), 1.0 / 16.0, 0.0)
    lines = jnp.dot(pick, narrow, precision=HIGH, preferred_element_type=F32)
    motion[:, 0:width] = lines[0:8]
    motion[:, width : width + 128] = fold_row(lines[8:9])
    motion[:, width + 128 : width + 256] = fold_row(lines[9:10])


def plate_first(scal, now, prev, n_rows):
    rows, cols = now.shape
    return pl.pallas_call(
        placed(functools.partial(plate_kernel, n_rows)),
        in_specs=[pl.BlockSpec(memory_space=pltpu.SMEM)] * 2
        + [pl.BlockSpec(memory_space=pltpu.VMEM)] * 2,
        out_specs=pl.BlockSpec(memory_space=pltpu.VMEM),
        out_shape=jax.ShapeDtypeStruct((8, cols // 4 + 256), F32),
        compiler_params=params(16),
        cost_estimate=cost(4 << 20),
    )(*scal, now, prev)


def carries(shape, strip, b):
    return (4 * strip + (iota(shape, 0) & 3) + b) >= 32


def to_plate_kernel(scal, came, motion, out):
    shift, strip = scal[1], scal[4]
    a, b = shift >> 5, shift & 31
    move = motion[...]
    width = move.shape[1] - 256
    carry = carries((8, width), strip, b)
    before = (4 * strip - 1 + b) >> 5
    behind = (4 * strip + 4 + b) >> 5

    def folded(block, lane):
        ok = jnp.where((block >= 0) & (block < 32), 1.0, 0.0).astype(F32)
        at = pl.multiple_of(8 * jnp.clip(block, 0, 31), 8)
        return came[pl.ds(at, 8), lane : lane + 128] * ok

    slab = scal[5]
    pair = jnp.clip((scal[0] - 1) >> 3, 0, 14)
    aside = (slab < pair) | (slab > pair + 1)
    for dest in range(16):
        at = pl.multiple_of(8 * (dest + a), 8)
        after = pl.multiple_of(8 * jnp.minimum(dest + a + 1, 31), 8)
        tile = jnp.where(carry, came[pl.ds(after, 8), 0:width], came[pl.ds(at, 8), 0:width])
        wants = aside & ((pair == dest) | (pair + 1 == dest))
        out[dest, :, 0:width] = jnp.where(wants, move[:, 0:width], tile)
        for n, block in ((0, dest + a + before), (1, dest + a + behind)):
            lane = width + 128 * n
            part = folded(block, lane)
            out[dest, :, lane : lane + 128] = jnp.where(wants, move[:, lane : lane + 128], part)


def to_plate(scal, came, motion):
    width = motion.shape[1] - 256
    return pl.pallas_call(
        placed(to_plate_kernel),
        in_specs=[pl.BlockSpec(memory_space=pltpu.SMEM)] * 2
        + [pl.BlockSpec(memory_space=pltpu.VMEM)] * 2,
        out_specs=pl.BlockSpec(memory_space=pltpu.VMEM),
        out_shape=jax.ShapeDtypeStruct((16, 8, width + 256), F32),
        compiler_params=params(16),
        cost_estimate=cost(2 << 20),
    )(*scal, came, motion)


def to_air_kernel(scal, came, motion, on_chip, off_chip, pressure, out, moves):
    shift, strip, slab = scal[1], scal[4], scal[5]
    a, b = shift >> 5, shift & 31
    width = pressure.shape[1] - 256
    pair = jnp.clip((scal[0] - 1) >> 3, 0, 14)
    pressure[...] = came[pair] + came[pair + 1]
    for src in range(16):
        moves[src] = came[src]
    moves[slab] = motion[...]
    moves[slab ^ 1] = on_chip[...]

    @pl.when((slab > 0) & (slab < 15))
    def _():
        moves[jnp.where((slab & 1) == 0, slab - 1, slab + 1)] = off_chip[...]

    shape = (8, width)
    carry = carries(shape, strip, b)
    row = iota(shape, 0)
    place = (4 * strip + (row & 3) + b) & 31
    first_field = row < 4
    before = (4 * strip - 1 + b) >> 5
    behind = (4 * strip + 4 + b) >> 5

    def part(src, lanes):
        ok = jnp.where((src >= 0) & (src < 16), 1.0, 0.0).astype(F32)
        return moves[jnp.clip(src, 0, 15), :, lanes] * ok

    def tile(block):
        lanes = slice(0, width)
        return jnp.where(carry, part(block - a - 1, lanes), part(block - a, lanes))

    def rim(block, spot):
        rows = jnp.where(first_field & (place == spot), tile(block), 0.0)
        return fold_row(jnp.sum(rows, axis=0, keepdims=True))

    none = jnp.zeros((8, 128), F32)
    for s in range(8):
        for k in range(4):
            at = slice(8 * k, 8 * k + 8)
            block = 4 * s + k
            out[s, at, 0:width] = tile(block)
            lanes = slice(width, width + 128)
            out[s, at, lanes] = part(block - a - before, lanes)
            lanes = slice(width + 128, width + 256)
            out[s, at, lanes] = part(block - a - behind, lanes)
        lanes = slice(width + 256, width + 384)
        out[s, 0:8, lanes] = rim(4 * s - 1, 31) if s > 0 else none
        out[s, 8:16, lanes] = rim(4 * s + 4, 0) if s < 7 else none
        out[s, 16:24, lanes] = none
        out[s, 24:32, lanes] = none


def to_air(scal, came, motion, on_chip, off_chip):
    width = motion.shape[1] - 256
    return pl.pallas_call(
        placed(to_air_kernel),
        in_specs=[pl.BlockSpec(memory_space=pltpu.SMEM)] * 2
        + [pl.BlockSpec(memory_space=pltpu.VMEM)] * 4,
        out_specs=[pl.BlockSpec(memory_space=pltpu.VMEM)] * 2,
        out_shape=[
            jax.ShapeDtypeStruct((8, width + 256), F32),
            jax.ShapeDtypeStruct((8, 32, width + 384), F32),
        ],
        scratch_shapes=[pltpu.VMEM((16, 8, width + 256), F32)],
        compiler_params=params(16),
        cost_estimate=cost(2 << 20),
    )(*scal, came, motion, on_chip, off_chip)


def add_corner_kernel(scal, field, on_chip, off_chip, out):
    t = pl.program_id(0)
    lower_core = (scal[5] & 1) == 0
    low = t < 2
    first_end = (t & 1) == 0
    near = jnp.where(jnp.logical_not(jnp.logical_xor(low, lower_core)), off_chip[...], on_chip[...])
    line = jnp.where(first_end, near[0:1], near[1:2])
    row = iota(out.shape[1:], 0)
    spot = jnp.where(first_end, 0, 7)
    out[0] = field[0] + jnp.where(row == spot, 0.18 * line, 0.0)


def add_corners(scal, field, on_chip, off_chip):
    depth, height, width = field.shape

    def where(t, *scal):
        return ((t >> 1) * (depth - 1), (t & 1) * (height // 8 - 1), 0)

    tile = pl.BlockSpec((1, 8, width), where)
    pack = pl.BlockSpec((8, width), lambda t, *scal: (0, 0))
    return pl.pallas_call(
        placed(add_corner_kernel),
        grid_spec=pltpu.PrefetchScalarGridSpec(
            num_scalar_prefetch=2, grid=(4,), in_specs=[tile, pack, pack], out_specs=tile
        ),
        out_shape=jax.ShapeDtypeStruct(field.shape, F32),
        input_output_aliases={2: 0},
        compiler_params=params(59),
        cost_estimate=cost(1 << 20),
    )(*scal, field, on_chip, off_chip)


def force_kernel(scal, field, came, press, out, q, r):
    level, shift, base = scal[0], scal[1], scal[2]
    t = pl.program_id(0)
    height, width = q.shape
    depth = 8
    b = shift & 31

    @pl.when(t == 0)
    def _():
        for k in range(height // 32):
            at = slice(32 * k, 32 * k + 32)
            tiles = [came[y, 8 * k : 8 * k + 8, :] for y in range(8)]
            now = jnp.concatenate([x[0:4, 0:width] for x in tiles], axis=0)
            later = []
            for y in range(8):
                own = tiles[y][4:8, 0:width]
                row = iota(own.shape, 0)
                top = unfold(tiles[(y - 1) % 8][:, width + 128 : width + 256])
                bottom = unfold(tiles[(y + 1) % 8][:, width : width + 128])
                own = own + jnp.where(row == 0, top, 0.0) + jnp.where(row == 3, bottom, 0.0)
                later.append(own)
            r[at, :] = pltpu.roll(now, b, 0)
            q[at, :] = pltpu.roll(jnp.concatenate(later, axis=0), b, 0)
        rim = came[0, 0:16, width + 256 : width + 384]
        for y in range(1, 8):
            rim = rim + came[y, 0:16, width + 256 : width + 384]
        above, below = unfold(rim[0:8]), unfold(rim[8:16])
        motion = r[...]
        around = left_right(motion) + up_down(motion, above, below)
        q[...] = (0.55 - 0.6) * motion + 0.15 * around + 0.5 * q[...] + press[...]

    z = jnp.clip(level - 1 + t - base, 0, depth - 1) + base

    def is_level(other):
        return jnp.where(z == other, 1.0, 0.0).astype(F32)

    wq = is_level(level) - is_level(level + 1)
    wr = 0.15 * (is_level(level - 1) - is_level(level + 2))
    out[0] = field[0] + wq * q[...] + wr * r[...]


def add_force(scal, field, came, press):
    depth, height, width = field.shape

    def where(t, *scal):
        scal = Place(*scal)
        return (jnp.clip(scal[0] - 1 + t - scal[2], 0, depth - 1), 0, 0)

    plane = pl.BlockSpec((1, height, width), where)
    return pl.pallas_call(
        placed(force_kernel),
        grid_spec=pltpu.PrefetchScalarGridSpec(
            num_scalar_prefetch=2,
            grid=(4,),
            in_specs=[
                plane,
                pl.BlockSpec((8, 32, width + 384), lambda t, *scal: (0, 0, 0)),
                pl.BlockSpec((height, width), lambda t, *scal: (0, 0)),
            ],
            out_specs=plane,
            scratch_shapes=[pltpu.VMEM((height, width), F32)] * 2,
        ),
        out_shape=jax.ShapeDtypeStruct(field.shape, F32),
        input_output_aliases={2: 0},
        compiler_params=params(24),
        cost_estimate=cost(4 << 20),
    )(*scal, field, came, press)


def plate_last_kernel(n_rows, scal, now, prev, below, above, pressure, motion, out):
    rows, cols = now.shape
    first = scal[3] * rows - 4
    width = motion.shape[1] - 256
    press = pressure[0:4, 0:width]
    lo = unfold(pressure[:, width : width + 128])
    hi = unfold(pressure[:, width + 128 : width + 256])
    around = left_right(press) + up_down(press, lo, hi) - 4.0 * press
    later = 2.0 * press + 0.3 * around + pressure[4:8, 0:width] - motion[0:4, 0:width]
    lines = jnp.concatenate([press, later, lo, hi, jnp.zeros((6, width), F32)], axis=0)
    spread = jnp.where((iota((128, 512), 1) >> 2) == iota((128, 512), 0), 1.0, 0.0)
    parts = [
        jnp.dot(lines[:, 128 * q : 128 * q + 128], spread, precision=HIGH, preferred_element_type=F32)
        for q in range(width // 128)
    ]
    wide = jnp.concatenate(parts, axis=1)
    e = iota((24, 16), 0)
    line = iota((24, 16), 1)
    source = jnp.where(e < 4, 8, jnp.where(e >= 20, 9, (e - 4) >> 2))
    pick = jnp.where(line == source, C_PRESS, 0.0)
    push = jnp.dot(pick, wide, precision=HIGH, preferred_element_type=F32)
    pick = jnp.where(iota((16, 16), 1) == 4 + (iota((16, 16), 0) >> 2), C_PRESS, 0.0)
    push_last = jnp.dot(pick, wide, precision=HIGH, preferred_element_type=F32)
    here = now[...]
    ext = jnp.concatenate([below[0:4, 0:cols], here, above[0:4, 0:cols]], axis=0)
    old = jnp.concatenate([below[4:8, 0:cols], prev[...], above[4:8, 0:cols]], axis=0)
    ok = inside_rows(ext.shape, first, n_rows)
    mid = jnp.where(ok, plate_step(ext, old, ok) + push, 0.0)
    inner = jnp.where(ok, flat_laplace(mid), 0.0)
    bend = flat_laplace(inner)[4 : 4 + rows]
    final = (2.0 * mid[4 : 4 + rows] - 0.99 * here - 0.04 * bend) * (1.0 / 1.01)
    out[...] = final + push_last


def plate_last(scal, now, prev, lo, hi, pressure, motion, n_rows):
    return pl.pallas_call(
        placed(functools.partial(plate_last_kernel, n_rows)),
        in_specs=[pl.BlockSpec(memory_space=pltpu.SMEM)] * 2
        + [pl.BlockSpec(memory_space=pltpu.VMEM)] * 6,
        out_specs=pl.BlockSpec(memory_space=pltpu.VMEM),
        out_shape=jax.ShapeDtypeStruct(now.shape, F32),
        compiler_params=params(16),
        cost_estimate=cost(4 << 20),
    )(*scal, now, prev, lo, hi, pressure, motion)


def neighbours(n):
    return [(i, i + 1) for i in range(n - 1)], [(i + 1, i) for i in range(n - 1)]


def shards(air_now, air_prev, plate_now, plate_prev, plate_level, plate_shift):
    depth, height, width = air_now.shape
    n_gz, n_gy = lax.axis_size("gz"), lax.axis_size("gy")
    n_rows = plate_now.shape[0] * n_gz * n_gy
    cols = plate_now.shape[1]
    scal = (plate_level, plate_shift)
    up_d, down_d = neighbours(n_gz * n_gy)

    first, last, sent = front(scal, air_now, air_prev, plate_now, plate_prev)
    came = lax.all_to_all(sent, "gy", 0, 0).reshape(256, width + 256)
    lo = lax.ppermute(last, ("gz", "gy"), up_d)
    hi = lax.ppermute(first, ("gz", "gy"), down_d)

    across = [(i, i + 1) for i in range(1, n_gz - 1, 2)]
    pairs_on = [(i, i ^ 1) for i in range(n_gz)]
    pairs_off = across + [(j, i) for i, j in across]
    motion = plate_first(scal, plate_now, plate_prev, n_rows)
    motion_on = lax.ppermute(motion, "gz", pairs_on)
    motion_off = lax.ppermute(motion, "gz", pairs_off)
    level, motion_on, motion_off = lax.optimization_barrier((plate_level, motion_on, motion_off))
    on_chip, off_chip = faces((level, plate_shift), air_now, air_prev)
    motion, on_chip, off_chip = lax.optimization_barrier((motion, on_chip, off_chip))
    on_chip = lax.ppermute(on_chip, "gz", pairs_on)
    off_chip = lax.ppermute(off_chip, "gz", pairs_off)

    came = lax.all_to_all(to_plate(scal, came, motion), "gz", 0, 0)
    came, lo, hi, on_chip, off_chip = lax.optimization_barrier((came, lo, hi, on_chip, off_chip))
    corner_on, corner_off = corners(scal, lo, hi, cols, width)
    corner_on = lax.ppermute(corner_on, "gz", pairs_on)
    corner_off = lax.ppermute(corner_off, "gz", pairs_off)
    pressure, sent = to_air(scal, came, motion, motion_on, motion_off)
    air_2, press_now = air_steps(
        scal, air_now, air_prev, on_chip, off_chip, lo, hi, cols
    )
    came = lax.all_to_all(sent, "gy", 0, 0)

    plate_2 = plate_last(scal, plate_now, plate_prev, lo, hi, pressure, motion, n_rows)
    air_2 = add_corners(scal, air_2, corner_on, corner_off)
    air_2 = add_force(scal, air_2, came, press_now)
    return (air_2, plate_2)


def solution(mesh):
    in_specs = (
        P("gz", "gy", None),
        P("gz", "gy", None),
        P(("gz", "gy"), None),
        P(("gz", "gy"), None),
        P(),
        P(),
    )
    out_specs = (P("gz", "gy", None), P(("gz", "gy"), None))
    return jax.shard_map(shards, mesh=mesh, in_specs=in_specs, out_specs=out_specs, check_vma=False)
```

```python
import functools

import jax
import jax.numpy as jnp
from jax import lax
from jax.experimental import pallas as pl
from jax.experimental.pallas import tpu as pltpu
from jax.sharding import PartitionSpec as P

F32 = jnp.float32
C_PRESS = 0.5 / 1.01
HIGH = lax.Precision.HIGHEST


def params(mib):
    return pltpu.CompilerParams(vmem_limit_bytes=mib << 20)


class Place:
    def __init__(self, level, shift):
        self.level, self.shift = level, shift

    def __getitem__(self, i):
        if i == 0:
            return self.level[0]
        if i == 1:
            return self.shift[0]
        slab, strip = lax.axis_index("gz"), lax.axis_index("gy")
        return {2: slab * 8, 3: slab * lax.axis_size("gy") + strip, 4: strip, 5: slab}[i]


def placed(kernel):
    def run(level, shift, *refs):
        kernel(Place(level, shift), *refs)

    return run


def cost(nbytes):
    return pl.CostEstimate(flops=nbytes, bytes_accessed=nbytes, transcendentals=0)


def iota(shape, axis):
    return lax.broadcasted_iota(jnp.int32, shape, axis)


def left_right(x):
    width = x.shape[1]
    col = iota(x.shape, 1)
    west = jnp.where(col == 0, 0.0, pltpu.roll(x, 1, 1))
    east = jnp.where(col == width - 1, 0.0, pltpu.roll(x, width - 1, 1))
    return west + east


def up_down(x, above, below):
    height = x.shape[0]
    row = iota(x.shape, 0)
    up = jnp.where(row == 0, above, pltpu.roll(x, 1, 0))
    down = jnp.where(row == height - 1, below, pltpu.roll(x, height - 1, 0))
    return up + down


def sweep(load, count, above, below, emit):
    here = load(0)
    shape = here.shape
    width = shape[1]
    row, col = iota(shape, 0), iota(shape, 1)
    top, bottom, left, right = row == 0, row == 7, col == 0, col == width - 1
    from_above = above
    up, down = pltpu.roll(here, 1, 0), pltpu.roll(here, 7, 0)
    for i in range(count):
        if i + 1 < count:
            later = load(i + 1)
            later_up, later_down = pltpu.roll(later, 1, 0), pltpu.roll(later, 7, 0)
            from_below = later_down
        else:
            from_below = below
        west = jnp.where(left, 0.0, pltpu.roll(here, 1, 1))
        east = jnp.where(right, 0.0, pltpu.roll(here, width - 1, 1))
        vertical = jnp.where(top, from_above, up) + jnp.where(bottom, from_below, down)
        emit(i, here, west + east + vertical)
        if i + 1 < count:
            from_above = up
            here, up, down = later, later_up, later_down


def pack_kernel(now0, now1, old0, old1, plate_now, plate_prev, first, last):
    rows = plate_now.shape[0]
    cols = plate_now.shape[1]
    width = now0.shape[2]
    for out, now, old, edge, inner, r in (
        (first, now0, old0, 0, 1, 0),
        (last, now1, old1, 7, 6, rows - 4),
    ):
        here = now[:, edge, :]
        depth = here.shape[0]
        out[0:4, 0:cols] = plate_now[r : r + 4, :]
        out[4:8, 0:cols] = plate_prev[r : r + 4, :]
        out[:, cols : cols + width] = here
        around = left_right(here) + up_down(here, 0.0, 0.0) + now[:, inner, :]
        out[:, cols + width : cols + 2 * width] = 0.2 * here - old[:, edge, :] + 0.3 * around


def face_kernel(scal, here, inner, old, on_chip, off_chip):
    height = here.shape[1]

    def one(out):
        def emit(i, x, around):
            at = slice(8 * i, 8 * i + 8)
            out[at, :] = x
            part = 0.2 * x - old[0, at, :] + 0.3 * (around + inner[0, at, :])
            out[height + 8 * i : height + 8 * i + 8, :] = part

        sweep(lambda i: here[0, 8 * i : 8 * i + 8, :], height // 8, 0.0, 0.0, emit)

    @pl.when(pl.program_id(0) == 0)
    def _():
        one(on_chip)

    @pl.when(pl.program_id(0) == 1)
    def _():
        one(off_chip)


def faces(scal, air_now, air_prev):
    depth, height, width = air_now.shape

    def plane(inner):
        def where(i, *scal):
            top = ((Place(*scal)[5] + i) & 1) == 0
            return (jnp.where(top, depth - 1 - inner, inner), 0, 0)

        return pl.BlockSpec((1, height, width), where)

    out = pl.BlockSpec((2 * height, width), lambda i, *scal: (0, 0))
    return pl.pallas_call(
        placed(face_kernel),
        grid_spec=pltpu.PrefetchScalarGridSpec(
            num_scalar_prefetch=2,
            grid=(2,),
            in_specs=[
                plane(0),
                plane(1),
                plane(0),
            ],
            out_specs=[out, out],
        ),
        out_shape=[jax.ShapeDtypeStruct((2 * height, width), F32)] * 2,
        compiler_params=params(59),
        cost_estimate=cost(5 << 20),
    )(*scal, air_now, air_now, air_prev)


def corner_kernel(scal, lo, hi, on_chip, off_chip):
    strip = scal[4]
    lower_core = (scal[5] & 1) == 0
    row = iota(on_chip.shape, 0)

    def ends(level):
        above = jnp.where(strip > 0, lo[level : level + 1, :], 0.0)
        below = jnp.where(strip < 7, hi[level : level + 1, :], 0.0)
        return jnp.where(row == 0, above, jnp.where(row == 1, below, 0.0))

    bottom, top = ends(0), ends(7)
    on_chip[...] = jnp.where(lower_core, top, bottom)
    off_chip[...] = jnp.where(lower_core, bottom, top)


def corners(scal, lo, hi, cols, width):
    edge = pl.BlockSpec((8, width), lambda i, *scal: (0, cols // width))
    out = pl.BlockSpec((8, width), lambda i, *scal: (0, 0))
    return pl.pallas_call(
        placed(corner_kernel),
        grid_spec=pltpu.PrefetchScalarGridSpec(
            num_scalar_prefetch=2, grid=(1,), in_specs=[edge, edge], out_specs=[out, out]
        ),
        out_shape=[jax.ShapeDtypeStruct((8, width), F32)] * 2,
        compiler_params=params(16),
        cost_estimate=cost(1 << 20),
    )(*scal, lo, hi)


def air_kernel(
    scal, now, prev, on_chip, off_chip, ylo, yhi,
    out, press, keep, mid, older, sems,
):
    level, shift, first, strip, slab = scal[0], scal[1], scal[2], scal[4], scal[5]
    t = pl.program_id(0)
    depth, height, width = now.shape
    strips = [slice(8 * i, 8 * i + 8) for i in range(height // 8)]
    y_lo = jnp.where(strip > 0, 1.0, 0.0).astype(F32)
    y_hi = jnp.where(strip < 7, 1.0, 0.0).astype(F32)
    lower_core = (slab & 1) == 0

    def zlo(first, count):
        at = slice(first, first + count)
        return jnp.where(lower_core, off_chip[at, :], on_chip[at, :])

    def zhi(first, count):
        at = slice(first, first + count)
        return jnp.where(lower_core, on_chip[at, :], off_chip[at, :])

    def fetch_now(z):
        return pltpu.make_async_copy(now.at[z], keep.at[z + 1], sems.at[0, z])

    def fetch_prev(z):
        return pltpu.make_async_copy(prev.at[z], older.at[z], sems.at[1, z])

    @pl.when(t == 0)
    def _():
        for z in range(depth):
            fetch_now(z).start()
            fetch_prev(z).start()

    @pl.when(t < depth)
    def _():
        fetch_now(t).wait()

    @pl.when((t >= 1) & (t <= depth))
    def _():
        fetch_prev(t - 1).wait()

    def outer(target, source, level, inside):
        inside = jnp.where(inside, 1.0, 0.0).astype(F32)
        for i, at in enumerate(strips):
            mid[target, at, :] = inside * (source(height + 8 * i, 8) + 0.3 * keep[level, at, :])

    @pl.when(t == 0)
    def _():
        for i, at in enumerate(strips):
            keep[0, at, :] = zlo(8 * i, 8)
            keep[depth + 1, at, :] = zhi(8 * i, 8)
        outer(0, zlo, 1, slab > 0)

    @pl.when(t == depth - 1)
    def _():
        outer(depth + 1, zhi, depth, slab < 15)

    @pl.when((t >= 1) & (t <= depth))
    def _():
        z = t - 1
        above = y_lo * ylo[pl.ds(z, 1), 0:width]
        below = y_hi * yhi[pl.ds(z, 1), 0:width]

        def emit(i, x, around):
            at = strips[i]
            total = around + keep[z, at, :] + keep[z + 2, at, :]
            mid[z + 1, at, :] = 0.2 * x - older[z, at, :] + 0.3 * total

        sweep(lambda i: keep[z + 1, strips[i], :], len(strips), above, below, emit)

    @pl.when(t >= 2)
    def _():
        z = t - 2

        def rim(rows, line):
            return rows[pl.ds(z, 1), width : 2 * width] + 0.3 * line

        above = y_lo * rim(ylo, keep[z + 1, 0:1, :])
        below = y_hi * rim(yhi, keep[z + 1, height - 1 : height, :])

        def emit(i, x, around):
            at = strips[i]
            total = around + mid[z, at, :] + mid[z + 2, at, :]
            out[0, at, :] = 0.2 * x - keep[z + 1, at, :] + 0.3 * total

        sweep(lambda i: mid[z + 1, strips[i], :], len(strips), above, below, emit)

    @pl.when(t == depth)
    def _():
        upper = jnp.clip(level + 1 - first, -1, depth) + 1
        lower = jnp.clip(level - first, -1, depth) + 1
        for i, at in enumerate(strips):
            y = iota((8, width), 0) + (strip * height + 8 * i - shift)
            gap = keep[upper, at, :] - keep[lower, at, :]
            press[at, :] = jnp.where((y >= 0) & (y < 512), (0.5 * C_PRESS) * gap, 0.0)


def air_steps(scal, now, prev, on_chip, off_chip, ylo, yhi, cols):
    depth, height, width = now.shape

    def plane(lag):
        return pl.BlockSpec(
            (1, height, width), lambda t, *scal: (jnp.clip(t - lag, 0, depth - 1), 0, 0)
        )

    whole = pl.BlockSpec(memory_space=pl.ANY)

    z_face = pl.BlockSpec((2 * height, width), lambda t, *scal: (0, 0))
    rows = pl.BlockSpec((8, 2 * width), lambda t, *scal: (0, cols // (2 * width)))
    return pl.pallas_call(
        placed(air_kernel),
        grid_spec=pltpu.PrefetchScalarGridSpec(
            num_scalar_prefetch=2,
            grid=(depth + 2,),
            in_specs=[whole, whole, z_face, z_face, rows, rows],
            out_specs=[
                plane(2),
                pl.BlockSpec((height, width), lambda t, *scal: (0, 0)),
            ],
            scratch_shapes=[pltpu.VMEM((depth + 2, height, width), F32)] * 2
            + [pltpu.VMEM(now.shape, F32), pltpu.SemaphoreType.DMA((2, depth))],
        ),
        out_shape=[
            jax.ShapeDtypeStruct(now.shape, F32),
            jax.ShapeDtypeStruct((height, width), F32),
        ],
        compiler_params=params(59),
        cost_estimate=cost(24 << 20),
    )(*scal, now, prev, on_chip, off_chip, ylo, yhi)


def fold_row(row):
    return jnp.concatenate([row[:, 128 * q : 128 * q + 128] for q in range(8)], axis=0)


def unfold(tile):
    return jnp.concatenate([tile[q : q + 1] for q in range(8)], axis=1)


def press_kernel(scal, up2, up1, at0, dn1, pup1, pat0, out):
    level, shift, base = scal[0], scal[1], scal[2]
    depth = 8
    width = up1.shape[2]

    def mine(z):
        return jnp.where((z >= base) & (z < base + depth), 1.0, 0.0).astype(F32)

    here = (level + 2 >= base) & (level - 1 < base + depth)

    @pl.when(jnp.logical_not(here))
    def _():
        out[...] = jnp.zeros(out.shape, F32)

    @pl.when(here)
    def _():
        m1, m0 = mine(level + 1), mine(level)
        m2, mm = mine(level + 2), mine(level - 1)
        b = shift & 31
        turn = (32 - b) & 31
        for k in range(up1.shape[1] // 32):
            at = slice(32 * k, 32 * k + 32)
            press = m1 * up1[0, at, :] - m0 * at0[0, at, :]
            vertical = m2 * up2[0, at, :] - 3.0 * press - mm * dn1[0, at, :]
            older = m1 * pup1[0, at, :] - m0 * pat0[0, at, :]
            r0 = pltpu.roll(press, turn, 0)
            r1 = pltpu.roll(0.3 * vertical - older, turn, 0)
            folded = [fold_row(r0[i : i + 1]) for i in range(32) if i & 3 in (0, 3)]
            for y in range(8):
                tile = slice(8 * k, 8 * k + 8)
                out[y, 8 * k : 8 * k + 4, 0:width] = r0[4 * y : 4 * y + 4]
                out[y, 8 * k + 4 : 8 * k + 8, 0:width] = r1[4 * y : 4 * y + 4]
                out[y, tile, width : width + 128] = folded[(2 * y - 1) % 16]
                out[y, tile, width + 128 : width + 256] = folded[(2 * y + 2) % 16]


def front_kernel(scal, *refs):
    pack_kernel(*refs[0:6], *refs[12:14])
    press_kernel(scal, *refs[6:12], refs[14])


def front(scal, air_now, air_prev, plate_now, plate_prev):
    depth, height, width = air_now.shape
    rows, cols = plate_now.shape
    low = pl.BlockSpec((depth, 8, width), lambda i, *scal: (0, 0, 0))
    high = pl.BlockSpec((depth, 8, width), lambda i, *scal: (0, height // 8 - 1, 0))
    plate = pl.BlockSpec((rows, cols), lambda i, *scal: (0, 0))
    pack = pl.BlockSpec((8, cols + 2 * width), lambda i, *scal: (0, 0))

    def plane(offset):
        def where(k, *scal):
            scal = Place(*scal)
            return (jnp.clip(scal[0] + offset - scal[2], 0, depth - 1), 0, 0)

        return pl.BlockSpec((1, height, width), where)

    return pl.pallas_call(
        placed(front_kernel),
        grid_spec=pltpu.PrefetchScalarGridSpec(
            num_scalar_prefetch=2,
            grid=(1,),
            in_specs=[low, high, low, high, plate, plate]
            + [plane(2), plane(1), plane(0), plane(-1), plane(1), plane(0)],
            out_specs=[pack, pack]
            + [pl.BlockSpec((8, 32, width + 256), lambda k, *scal: (0, 0, 0))],
        ),
        out_shape=[jax.ShapeDtypeStruct((8, cols + 2 * width), F32)] * 2
        + [jax.ShapeDtypeStruct((8, 32, width + 256), F32)],
        compiler_params=params(59),
        cost_estimate=cost(6 << 20),
    )(
        *scal,
        *(air_now, air_now, air_prev, air_prev, plate_now, plate_prev),
        *(air_now, air_now, air_now, air_now, air_prev, air_prev),
    )


def flat_laplace(x):
    height = x.shape[0]
    return left_right(x) + pltpu.roll(x, 1, 0) + pltpu.roll(x, height - 1, 0) - 4.0 * x


def inside_rows(shape, first, last_row):
    row = iota(shape, 0) + first
    return (row >= 0) & (row < last_row)


def plate_step(ext, old, ok):
    inner = jnp.where(ok, flat_laplace(ext), 0.0)
    bend = flat_laplace(inner)
    return (2.0 * ext - 0.99 * old - 0.04 * bend) * (1.0 / 1.01)


def plate_kernel(n_rows, scal, now, prev, motion):
    rows, cols = now.shape
    first = scal[3] * rows - 4
    here = now[...]
    far = jnp.zeros((4, cols), F32)
    ext = jnp.concatenate([far, here, far], axis=0)
    old = jnp.concatenate([far, prev[...], far], axis=0)
    ok = inside_rows(ext.shape, first, n_rows)
    nxt = jnp.where(ok, plate_step(ext, old, ok), 0.0) - ext
    both = jnp.concatenate([here - prev[...], nxt], axis=0)
    fold = jnp.where((iota((512, 128), 0) >> 2) == iota((512, 128), 1), 1.0, 0.0)
    parts = [
        jnp.dot(both[:, 512 * q : 512 * q + 512], fold, precision=HIGH, preferred_element_type=F32)
        for q in range(cols // 512)
    ]
    narrow = jnp.concatenate(parts, axis=1)
    width = narrow.shape[1]
    row = iota((16, 40), 0)
    source = jnp.where(row < 4, row, jnp.where(row < 8, row + 1, jnp.where(row == 8, 4, 9)))
    pick = jnp.where((source == (iota((16, 40), 1) >> 2)) & (row < 10), 1.0 / 16.0, 0.0)
    lines = jnp.dot(pick, narrow, precision=HIGH, preferred_element_type=F32)
    motion[:, 0:width] = lines[0:8]
    motion[:, width : width + 128] = fold_row(lines[8:9])
    motion[:, width + 128 : width + 256] = fold_row(lines[9:10])


def plate_first(scal, now, prev, n_rows):
    rows, cols = now.shape
    return pl.pallas_call(
        placed(functools.partial(plate_kernel, n_rows)),
        in_specs=[pl.BlockSpec(memory_space=pltpu.SMEM)] * 2
        + [pl.BlockSpec(memory_space=pltpu.VMEM)] * 2,
        out_specs=pl.BlockSpec(memory_space=pltpu.VMEM),
        out_shape=jax.ShapeDtypeStruct((8, cols // 4 + 256), F32),
        compiler_params=params(16),
        cost_estimate=cost(4 << 20),
    )(*scal, now, prev)


def carries(shape, strip, b):
    return (4 * strip + (iota(shape, 0) & 3) + b) >= 32


def to_plate_kernel(scal, came, motion, out):
    shift, strip = scal[1], scal[4]
    a, b = shift >> 5, shift & 31
    move = motion[...]
    width = move.shape[1] - 256
    carry = carries((8, width), strip, b)
    before = (4 * strip - 1 + b) >> 5
    behind = (4 * strip + 4 + b) >> 5

    def folded(block, lane):
        ok = jnp.where((block >= 0) & (block < 32), 1.0, 0.0).astype(F32)
        at = pl.multiple_of(8 * jnp.clip(block, 0, 31), 8)
        return came[pl.ds(at, 8), lane : lane + 128] * ok

    slab = scal[5]
    pair = jnp.clip((scal[0] - 1) >> 3, 0, 14)
    aside = (slab < pair) | (slab > pair + 1)
    for dest in range(16):
        at = pl.multiple_of(8 * (dest + a), 8)
        after = pl.multiple_of(8 * jnp.minimum(dest + a + 1, 31), 8)
        tile = jnp.where(carry, came[pl.ds(after, 8), 0:width], came[pl.ds(at, 8), 0:width])
        wants = aside & ((pair == dest) | (pair + 1 == dest))
        out[dest, :, 0:width] = jnp.where(wants, move[:, 0:width], tile)
        for n, block in ((0, dest + a + before), (1, dest + a + behind)):
            lane = width + 128 * n
            part = folded(block, lane)
            out[dest, :, lane : lane + 128] = jnp.where(wants, move[:, lane : lane + 128], part)


def to_plate(scal, came, motion):
    width = motion.shape[1] - 256
    return pl.pallas_call(
        placed(to_plate_kernel),
        in_specs=[pl.BlockSpec(memory_space=pltpu.SMEM)] * 2
        + [pl.BlockSpec(memory_space=pltpu.VMEM)] * 2,
        out_specs=pl.BlockSpec(memory_space=pltpu.VMEM),
        out_shape=jax.ShapeDtypeStruct((16, 8, width + 256), F32),
        compiler_params=params(16),
        cost_estimate=cost(2 << 20),
    )(*scal, came, motion)


def to_air_kernel(scal, came, motion, on_chip, off_chip, pressure, out, moves):
    shift, strip, slab = scal[1], scal[4], scal[5]
    a, b = shift >> 5, shift & 31
    width = pressure.shape[1] - 256
    pair = jnp.clip((scal[0] - 1) >> 3, 0, 14)
    pressure[...] = came[pair] + came[pair + 1]
    for src in range(16):
        moves[src] = came[src]
    moves[slab] = motion[...]
    moves[slab ^ 1] = on_chip[...]

    @pl.when((slab > 0) & (slab < 15))
    def _():
        moves[jnp.where((slab & 1) == 0, slab - 1, slab + 1)] = off_chip[...]

    shape = (8, width)
    carry = carries(shape, strip, b)
    row = iota(shape, 0)
    place = (4 * strip + (row & 3) + b) & 31
    first_field = row < 4
    before = (4 * strip - 1 + b) >> 5
    behind = (4 * strip + 4 + b) >> 5

    def part(src, lanes):
        ok = jnp.where((src >= 0) & (src < 16), 1.0, 0.0).astype(F32)
        return moves[jnp.clip(src, 0, 15), :, lanes] * ok

    def tile(block):
        lanes = slice(0, width)
        return jnp.where(carry, part(block - a - 1, lanes), part(block - a, lanes))

    def rim(block, spot):
        rows = jnp.where(first_field & (place == spot), tile(block), 0.0)
        return fold_row(jnp.sum(rows, axis=0, keepdims=True))

    none = jnp.zeros((8, 128), F32)
    for s in range(8):
        for k in range(4):
            at = slice(8 * k, 8 * k + 8)
            block = 4 * s + k
            out[s, at, 0:width] = tile(block)
            lanes = slice(width, width + 128)
            out[s, at, lanes] = part(block - a - before, lanes)
            lanes = slice(width + 128, width + 256)
            out[s, at, lanes] = part(block - a - behind, lanes)
        lanes = slice(width + 256, width + 384)
        out[s, 0:8, lanes] = rim(4 * s - 1, 31) if s > 0 else none
        out[s, 8:16, lanes] = rim(4 * s + 4, 0) if s < 7 else none
        out[s, 16:24, lanes] = none
        out[s, 24:32, lanes] = none


def to_air(scal, came, motion, on_chip, off_chip):
    width = motion.shape[1] - 256
    return pl.pallas_call(
        placed(to_air_kernel),
        in_specs=[pl.BlockSpec(memory_space=pltpu.SMEM)] * 2
        + [pl.BlockSpec(memory_space=pltpu.VMEM)] * 4,
        out_specs=[pl.BlockSpec(memory_space=pltpu.VMEM)] * 2,
        out_shape=[
            jax.ShapeDtypeStruct((8, width + 256), F32),
            jax.ShapeDtypeStruct((8, 32, width + 384), F32),
        ],
        scratch_shapes=[pltpu.VMEM((16, 8, width + 256), F32)],
        compiler_params=params(16),
        cost_estimate=cost(2 << 20),
    )(*scal, came, motion, on_chip, off_chip)


def add_corner_kernel(scal, field, on_chip, off_chip, out):
    lower_core = (scal[5] & 1) == 0
    first_end = pl.program_id(0) == 0
    depth = field.shape[0]
    row = iota(field.shape[1:], 0)
    spot = jnp.where(first_end, 0, 7)

    def line(near):
        return jnp.where(row == spot, 0.18 * jnp.where(first_end, near[0:1], near[1:2]), 0.0)

    below = line(jnp.where(lower_core, off_chip[...], on_chip[...]))
    above = line(jnp.where(lower_core, on_chip[...], off_chip[...]))
    out[0] = field[0] + below
    for z in range(1, depth - 1):
        out[z] = field[z]
    out[depth - 1] = field[depth - 1] + above


def add_corners(scal, field, on_chip, off_chip):
    depth, height, width = field.shape

    tile = pl.BlockSpec((depth, 8, width), lambda t, *scal: (0, t * (height // 8 - 1), 0))
    pack = pl.BlockSpec((8, width), lambda t, *scal: (0, 0))
    return pl.pallas_call(
        placed(add_corner_kernel),
        grid_spec=pltpu.PrefetchScalarGridSpec(
            num_scalar_prefetch=2, grid=(2,), in_specs=[tile, pack, pack], out_specs=tile
        ),
        out_shape=jax.ShapeDtypeStruct(field.shape, F32),
        input_output_aliases={2: 0},
        compiler_params=params(59),
        cost_estimate=cost(1 << 20),
    )(*scal, field, on_chip, off_chip)


def force_kernel(scal, field, came, press, out, q, r):
    level, shift, base = scal[0], scal[1], scal[2]
    t = pl.program_id(0)
    height, width = q.shape
    depth = 8
    b = shift & 31

    @pl.when(t == 0)
    def _():
        for k in range(height // 32):
            at = slice(32 * k, 32 * k + 32)
            tiles = [came[y, 8 * k : 8 * k + 8, :] for y in range(8)]
            now = jnp.concatenate([x[0:4, 0:width] for x in tiles], axis=0)
            later = []
            for y in range(8):
                own = tiles[y][4:8, 0:width]
                row = iota(own.shape, 0)
                top = unfold(tiles[(y - 1) % 8][:, width + 128 : width + 256])
                bottom = unfold(tiles[(y + 1) % 8][:, width : width + 128])
                own = own + jnp.where(row == 0, top, 0.0) + jnp.where(row == 3, bottom, 0.0)
                later.append(own)
            r[at, :] = pltpu.roll(now, b, 0)
            q[at, :] = pltpu.roll(jnp.concatenate(later, axis=0), b, 0)
        rim = came[0, 0:16, width + 256 : width + 384]
        for y in range(1, 8):
            rim = rim + came[y, 0:16, width + 256 : width + 384]
        above, below = unfold(rim[0:8]), unfold(rim[8:16])
        motion = r[...]
        around = left_right(motion) + up_down(motion, above, below)
        q[...] = (0.55 - 0.6) * motion + 0.15 * around + 0.5 * q[...] + press[...]

    z = jnp.clip(level - 1 + t - base, 0, depth - 1) + base

    def is_level(other):
        return jnp.where(z == other, 1.0, 0.0).astype(F32)

    wq = is_level(level) - is_level(level + 1)
    wr = 0.15 * (is_level(level - 1) - is_level(level + 2))
    out[0] = field[0] + wq * q[...] + wr * r[...]


def add_force(scal, field, came, press):
    depth, height, width = field.shape

    def where(t, *scal):
        scal = Place(*scal)
        return (jnp.clip(scal[0] - 1 + t - scal[2], 0, depth - 1), 0, 0)

    plane = pl.BlockSpec((1, height, width), where)
    return pl.pallas_call(
        placed(force_kernel),
        grid_spec=pltpu.PrefetchScalarGridSpec(
            num_scalar_prefetch=2,
            grid=(4,),
            in_specs=[
                plane,
                pl.BlockSpec((8, 32, width + 384), lambda t, *scal: (0, 0, 0)),
                pl.BlockSpec((height, width), lambda t, *scal: (0, 0)),
            ],
            out_specs=plane,
            scratch_shapes=[pltpu.VMEM((height, width), F32)] * 2,
        ),
        out_shape=jax.ShapeDtypeStruct(field.shape, F32),
        input_output_aliases={2: 0},
        compiler_params=params(24),
        cost_estimate=cost(4 << 20),
    )(*scal, field, came, press)


def plate_last_kernel(n_rows, scal, now, prev, below, above, pressure, motion, out):
    rows, cols = now.shape
    first = scal[3] * rows - 4
    width = motion.shape[1] - 256
    press = pressure[0:4, 0:width]
    lo = unfold(pressure[:, width : width + 128])
    hi = unfold(pressure[:, width + 128 : width + 256])
    around = left_right(press) + up_down(press, lo, hi) - 4.0 * press
    later = 2.0 * press + 0.3 * around + pressure[4:8, 0:width] - motion[0:4, 0:width]
    lines = jnp.concatenate([press, later, lo, hi, jnp.zeros((6, width), F32)], axis=0)
    spread = jnp.where((iota((128, 512), 1) >> 2) == iota((128, 512), 0), 1.0, 0.0)
    parts = [
        jnp.dot(lines[:, 128 * q : 128 * q + 128], spread, precision=HIGH, preferred_element_type=F32)
        for q in range(width // 128)
    ]
    wide = jnp.concatenate(parts, axis=1)
    e = iota((24, 16), 0)
    line = iota((24, 16), 1)
    source = jnp.where(e < 4, 8, jnp.where(e >= 20, 9, (e - 4) >> 2))
    pick = jnp.where(line == source, C_PRESS, 0.0)
    push = jnp.dot(pick, wide, precision=HIGH, preferred_element_type=F32)
    pick = jnp.where(iota((16, 16), 1) == 4 + (iota((16, 16), 0) >> 2), C_PRESS, 0.0)
    push_last = jnp.dot(pick, wide, precision=HIGH, preferred_element_type=F32)
    here = now[...]
    ext = jnp.concatenate([below[0:4, 0:cols], here, above[0:4, 0:cols]], axis=0)
    old = jnp.concatenate([below[4:8, 0:cols], prev[...], above[4:8, 0:cols]], axis=0)
    ok = inside_rows(ext.shape, first, n_rows)
    mid = jnp.where(ok, plate_step(ext, old, ok) + push, 0.0)
    inner = jnp.where(ok, flat_laplace(mid), 0.0)
    bend = flat_laplace(inner)[4 : 4 + rows]
    final = (2.0 * mid[4 : 4 + rows] - 0.99 * here - 0.04 * bend) * (1.0 / 1.01)
    out[...] = final + push_last


def plate_last(scal, now, prev, lo, hi, pressure, motion, n_rows):
    return pl.pallas_call(
        placed(functools.partial(plate_last_kernel, n_rows)),
        in_specs=[pl.BlockSpec(memory_space=pltpu.SMEM)] * 2
        + [pl.BlockSpec(memory_space=pltpu.VMEM)] * 6,
        out_specs=pl.BlockSpec(memory_space=pltpu.VMEM),
        out_shape=jax.ShapeDtypeStruct(now.shape, F32),
        compiler_params=params(16),
        cost_estimate=cost(4 << 20),
    )(*scal, now, prev, lo, hi, pressure, motion)


def neighbours(n):
    return [(i, i + 1) for i in range(n - 1)], [(i + 1, i) for i in range(n - 1)]


def shards(air_now, air_prev, plate_now, plate_prev, plate_level, plate_shift):
    depth, height, width = air_now.shape
    n_gz, n_gy = lax.axis_size("gz"), lax.axis_size("gy")
    n_rows = plate_now.shape[0] * n_gz * n_gy
    cols = plate_now.shape[1]
    scal = (plate_level, plate_shift)
    up_d, down_d = neighbours(n_gz * n_gy)

    first, last, sent = front(scal, air_now, air_prev, plate_now, plate_prev)
    came = lax.all_to_all(sent, "gy", 0, 0).reshape(256, width + 256)
    lo = lax.ppermute(last, ("gz", "gy"), up_d)
    hi = lax.ppermute(first, ("gz", "gy"), down_d)

    across = [(i, i + 1) for i in range(1, n_gz - 1, 2)]
    pairs_on = [(i, i ^ 1) for i in range(n_gz)]
    pairs_off = across + [(j, i) for i, j in across]
    motion = plate_first(scal, plate_now, plate_prev, n_rows)
    motion_on = lax.ppermute(motion, "gz", pairs_on)
    motion_off = lax.ppermute(motion, "gz", pairs_off)
    level, motion_on, motion_off = lax.optimization_barrier((plate_level, motion_on, motion_off))
    on_chip, off_chip = faces((level, plate_shift), air_now, air_prev)
    motion, on_chip, off_chip = lax.optimization_barrier((motion, on_chip, off_chip))
    on_chip = lax.ppermute(on_chip, "gz", pairs_on)
    off_chip = lax.ppermute(off_chip, "gz", pairs_off)

    came = lax.all_to_all(to_plate(scal, came, motion), "gz", 0, 0)
    came, lo, hi, on_chip, off_chip = lax.optimization_barrier((came, lo, hi, on_chip, off_chip))
    corner_on, corner_off = corners(scal, lo, hi, cols, width)
    corner_on = lax.ppermute(corner_on, "gz", pairs_on)
    corner_off = lax.ppermute(corner_off, "gz", pairs_off)
    pressure, sent = to_air(scal, came, motion, motion_on, motion_off)
    air_2, press_now = air_steps(
        scal, air_now, air_prev, on_chip, off_chip, lo, hi, cols
    )
    came = lax.all_to_all(sent, "gy", 0, 0)

    plate_2 = plate_last(scal, plate_now, plate_prev, lo, hi, pressure, motion, n_rows)
    air_2 = add_corners(scal, air_2, corner_on, corner_off)
    air_2 = add_force(scal, air_2, came, press_now)
    return (air_2, plate_2)


def solution(mesh):
    in_specs = (
        P("gz", "gy", None),
        P("gz", "gy", None),
        P(("gz", "gy"), None),
        P(("gz", "gy"), None),
        P(),
        P(),
    )
    out_specs = (P("gz", "gy", None), P(("gz", "gy"), None))
    return jax.shard_map(shards, mesh=mesh, in_specs=in_specs, out_specs=out_specs, check_vma=False)
```

```python
import functools

import jax
import jax.numpy as jnp
from jax import lax
from jax.experimental import pallas as pl
from jax.experimental.pallas import tpu as pltpu
from jax.sharding import PartitionSpec as P

F32 = jnp.float32
C_PRESS = 0.5 / 1.01
HIGH = lax.Precision.HIGHEST


def params(mib):
    return pltpu.CompilerParams(vmem_limit_bytes=mib << 20)


class Place:
    def __init__(self, level, shift):
        self.level, self.shift = level, shift

    def __getitem__(self, i):
        if i == 0:
            return self.level[0]
        if i == 1:
            return self.shift[0]
        slab, strip = lax.axis_index("gz"), lax.axis_index("gy")
        return {2: slab * 8, 3: slab * lax.axis_size("gy") + strip, 4: strip, 5: slab}[i]


def placed(kernel):
    def run(level, shift, *refs):
        kernel(Place(level, shift), *refs)

    return run


def cost(nbytes):
    return pl.CostEstimate(flops=nbytes, bytes_accessed=nbytes, transcendentals=0)


def iota(shape, axis):
    return lax.broadcasted_iota(jnp.int32, shape, axis)


def left_right(x):
    width = x.shape[1]
    col = iota(x.shape, 1)
    west = jnp.where(col == 0, 0.0, pltpu.roll(x, 1, 1))
    east = jnp.where(col == width - 1, 0.0, pltpu.roll(x, width - 1, 1))
    return west + east


def up_down(x, above, below):
    height = x.shape[0]
    row = iota(x.shape, 0)
    up = jnp.where(row == 0, above, pltpu.roll(x, 1, 0))
    down = jnp.where(row == height - 1, below, pltpu.roll(x, height - 1, 0))
    return up + down


def sweep(load, count, above, below, emit):
    here = load(0)
    shape = here.shape
    width = shape[1]
    row, col = iota(shape, 0), iota(shape, 1)
    top, bottom, left, right = row == 0, row == 7, col == 0, col == width - 1
    from_above = above
    up, down = pltpu.roll(here, 1, 0), pltpu.roll(here, 7, 0)
    for i in range(count):
        if i + 1 < count:
            later = load(i + 1)
            later_up, later_down = pltpu.roll(later, 1, 0), pltpu.roll(later, 7, 0)
            from_below = later_down
        else:
            from_below = below
        west = jnp.where(left, 0.0, pltpu.roll(here, 1, 1))
        east = jnp.where(right, 0.0, pltpu.roll(here, width - 1, 1))
        vertical = jnp.where(top, from_above, up) + jnp.where(bottom, from_below, down)
        emit(i, here, west + east + vertical)
        if i + 1 < count:
            from_above = up
            here, up, down = later, later_up, later_down


def pack_kernel(now0, now1, old0, old1, plate_now, plate_prev, first, last):
    rows = plate_now.shape[0]
    cols = plate_now.shape[1]
    width = now0.shape[2]
    for out, now, old, edge, inner, r in (
        (first, now0, old0, 0, 1, 0),
        (last, now1, old1, 7, 6, rows - 4),
    ):
        here = now[:, edge, :]
        depth = here.shape[0]
        out[0:4, 0:cols] = plate_now[r : r + 4, :]
        out[4:8, 0:cols] = plate_prev[r : r + 4, :]
        out[:, cols : cols + width] = here
        around = left_right(here) + up_down(here, 0.0, 0.0) + now[:, inner, :]
        out[:, cols + width : cols + 2 * width] = 0.2 * here - old[:, edge, :] + 0.3 * around


def face_kernel(scal, here, inner, old, on_chip, off_chip):
    height = here.shape[1]

    def one(out):
        def emit(i, x, around):
            at = slice(8 * i, 8 * i + 8)
            out[at, :] = x
            part = 0.2 * x - old[0, at, :] + 0.3 * (around + inner[0, at, :])
            out[height + 8 * i : height + 8 * i + 8, :] = part

        sweep(lambda i: here[0, 8 * i : 8 * i + 8, :], height // 8, 0.0, 0.0, emit)

    @pl.when(pl.program_id(0) == 0)
    def _():
        one(on_chip)

    @pl.when(pl.program_id(0) == 1)
    def _():
        one(off_chip)


def faces(scal, air_now, air_prev):
    depth, height, width = air_now.shape

    def plane(inner):
        def where(i, *scal):
            top = ((Place(*scal)[5] + i) & 1) == 0
            return (jnp.where(top, depth - 1 - inner, inner), 0, 0)

        return pl.BlockSpec((1, height, width), where)

    out = pl.BlockSpec((2 * height, width), lambda i, *scal: (0, 0))
    return pl.pallas_call(
        placed(face_kernel),
        grid_spec=pltpu.PrefetchScalarGridSpec(
            num_scalar_prefetch=2,
            grid=(2,),
            in_specs=[
                plane(0),
                plane(1),
                plane(0),
            ],
            out_specs=[out, out],
        ),
        out_shape=[jax.ShapeDtypeStruct((2 * height, width), F32)] * 2,
        compiler_params=params(59),
        cost_estimate=cost(5 << 20),
    )(*scal, air_now, air_now, air_prev)


def corner_kernel(scal, lo, hi, on_chip, off_chip):
    strip = scal[4]
    lower_core = (scal[5] & 1) == 0
    row = iota(on_chip.shape, 0)

    def ends(level):
        above = jnp.where(strip > 0, lo[level : level + 1, :], 0.0)
        below = jnp.where(strip < 7, hi[level : level + 1, :], 0.0)
        return jnp.where(row == 0, above, jnp.where(row == 1, below, 0.0))

    bottom, top = ends(0), ends(7)
    on_chip[...] = jnp.where(lower_core, top, bottom)
    off_chip[...] = jnp.where(lower_core, bottom, top)


def corners(scal, lo, hi, cols, width):
    edge = pl.BlockSpec((8, width), lambda i, *scal: (0, cols // width))
    out = pl.BlockSpec((8, width), lambda i, *scal: (0, 0))
    return pl.pallas_call(
        placed(corner_kernel),
        grid_spec=pltpu.PrefetchScalarGridSpec(
            num_scalar_prefetch=2, grid=(1,), in_specs=[edge, edge], out_specs=[out, out]
        ),
        out_shape=[jax.ShapeDtypeStruct((8, width), F32)] * 2,
        compiler_params=params(16),
        cost_estimate=cost(1 << 20),
    )(*scal, lo, hi)


def air_kernel(
    scal, now, prev, on_chip, off_chip, ylo, yhi,
    out, press, keep, mid, older, sems,
):
    level, shift, first, strip, slab = scal[0], scal[1], scal[2], scal[4], scal[5]
    t = pl.program_id(0)
    depth, height, width = now.shape
    strips = [slice(8 * i, 8 * i + 8) for i in range(height // 8)]
    y_lo = jnp.where(strip > 0, 1.0, 0.0).astype(F32)
    y_hi = jnp.where(strip < 7, 1.0, 0.0).astype(F32)
    lower_core = (slab & 1) == 0

    def zlo(first, count):
        at = slice(first, first + count)
        return jnp.where(lower_core, off_chip[at, :], on_chip[at, :])

    def zhi(first, count):
        at = slice(first, first + count)
        return jnp.where(lower_core, on_chip[at, :], off_chip[at, :])

    def fetch_now(z):
        return pltpu.make_async_copy(now.at[z], keep.at[z + 1], sems.at[0, z])

    def fetch_prev(z):
        return pltpu.make_async_copy(prev.at[z], older.at[z], sems.at[1, z])

    @pl.when(t == 0)
    def _():
        for z in range(depth):
            fetch_now(z).start()
            fetch_prev(z).start()

    pairs = depth // 2

    @pl.when(t == 0)
    def _():
        fetch_now(0).wait()

    @pl.when(t < pairs)
    def _():
        fetch_now(2 * t + 1).wait()
        fetch_prev(2 * t).wait()
        fetch_prev(2 * t + 1).wait()

    @pl.when(t < pairs - 1)
    def _():
        fetch_now(2 * t + 2).wait()

    def outer(target, source, level, inside):
        inside = jnp.where(inside, 1.0, 0.0).astype(F32)
        for i, at in enumerate(strips):
            mid[target, at, :] = inside * (source(height + 8 * i, 8) + 0.3 * keep[level, at, :])

    @pl.when(t == 0)
    def _():
        for i, at in enumerate(strips):
            keep[0, at, :] = zlo(8 * i, 8)
            keep[depth + 1, at, :] = zhi(8 * i, 8)
        outer(0, zlo, 1, slab > 0)

    @pl.when(t == pairs - 1)
    def _():
        outer(depth + 1, zhi, depth, slab < 15)

    def first_step(z):
        above = y_lo * ylo[pl.ds(z, 1), 0:width]
        below = y_hi * yhi[pl.ds(z, 1), 0:width]

        def emit(i, x, around):
            at = strips[i]
            total = around + keep[z, at, :] + keep[z + 2, at, :]
            mid[z + 1, at, :] = 0.2 * x - older[z, at, :] + 0.3 * total

        sweep(lambda i: keep[z + 1, strips[i], :], len(strips), above, below, emit)

    def second_step(z, slot):
        def rim(rows, line):
            return rows[pl.ds(z, 1), width : 2 * width] + 0.3 * line

        above = y_lo * rim(ylo, keep[z + 1, 0:1, :])
        below = y_hi * rim(yhi, keep[z + 1, height - 1 : height, :])

        def emit(i, x, around):
            at = strips[i]
            total = around + mid[z, at, :] + mid[z + 2, at, :]
            out[slot, at, :] = 0.2 * x - keep[z + 1, at, :] + 0.3 * total

        sweep(lambda i: mid[z + 1, strips[i], :], len(strips), above, below, emit)

    @pl.when(t < pairs)
    def _():
        first_step(2 * t)
        first_step(2 * t + 1)

    @pl.when(t >= 1)
    def _():
        second_step(2 * t - 2, 0)
        second_step(2 * t - 1, 1)

    @pl.when(t == pairs)
    def _():
        upper = jnp.clip(level + 1 - first, -1, depth) + 1
        lower = jnp.clip(level - first, -1, depth) + 1
        for i, at in enumerate(strips):
            y = iota((8, width), 0) + (strip * height + 8 * i - shift)
            gap = keep[upper, at, :] - keep[lower, at, :]
            press[at, :] = jnp.where((y >= 0) & (y < 512), (0.5 * C_PRESS) * gap, 0.0)


def air_steps(scal, now, prev, on_chip, off_chip, ylo, yhi, cols):
    depth, height, width = now.shape

    pair = pl.BlockSpec(
        (2, height, width), lambda t, *scal: (jnp.clip(t - 1, 0, depth // 2 - 1), 0, 0)
    )
    whole = pl.BlockSpec(memory_space=pl.ANY)

    z_face = pl.BlockSpec((2 * height, width), lambda t, *scal: (0, 0))
    rows = pl.BlockSpec((8, 2 * width), lambda t, *scal: (0, cols // (2 * width)))
    return pl.pallas_call(
        placed(air_kernel),
        grid_spec=pltpu.PrefetchScalarGridSpec(
            num_scalar_prefetch=2,
            grid=(depth // 2 + 1,),
            in_specs=[whole, whole, z_face, z_face, rows, rows],
            out_specs=[
                pair,
                pl.BlockSpec((height, width), lambda t, *scal: (0, 0)),
            ],
            scratch_shapes=[pltpu.VMEM((depth + 2, height, width), F32)] * 2
            + [pltpu.VMEM(now.shape, F32), pltpu.SemaphoreType.DMA((2, depth))],
        ),
        out_shape=[
            jax.ShapeDtypeStruct(now.shape, F32),
            jax.ShapeDtypeStruct((height, width), F32),
        ],
        compiler_params=params(59),
        cost_estimate=cost(24 << 20),
    )(*scal, now, prev, on_chip, off_chip, ylo, yhi)


def fold_row(row):
    return jnp.concatenate([row[:, 128 * q : 128 * q + 128] for q in range(8)], axis=0)


def unfold(tile):
    return jnp.concatenate([tile[q : q + 1] for q in range(8)], axis=1)


def press_kernel(scal, up2, up1, at0, dn1, pup1, pat0, out):
    level, shift, base = scal[0], scal[1], scal[2]
    depth = 8
    width = up1.shape[2]

    def mine(z):
        return jnp.where((z >= base) & (z < base + depth), 1.0, 0.0).astype(F32)

    here = (level + 2 >= base) & (level - 1 < base + depth)

    @pl.when(jnp.logical_not(here))
    def _():
        out[...] = jnp.zeros(out.shape, F32)

    @pl.when(here)
    def _():
        m1, m0 = mine(level + 1), mine(level)
        m2, mm = mine(level + 2), mine(level - 1)
        b = shift & 31
        turn = (32 - b) & 31
        for k in range(up1.shape[1] // 32):
            at = slice(32 * k, 32 * k + 32)
            press = m1 * up1[0, at, :] - m0 * at0[0, at, :]
            vertical = m2 * up2[0, at, :] - 3.0 * press - mm * dn1[0, at, :]
            older = m1 * pup1[0, at, :] - m0 * pat0[0, at, :]
            r0 = pltpu.roll(press, turn, 0)
            r1 = pltpu.roll(0.3 * vertical - older, turn, 0)
            folded = [fold_row(r0[i : i + 1]) for i in range(32) if i & 3 in (0, 3)]
            for y in range(8):
                tile = slice(8 * k, 8 * k + 8)
                out[y, 8 * k : 8 * k + 4, 0:width] = r0[4 * y : 4 * y + 4]
                out[y, 8 * k + 4 : 8 * k + 8, 0:width] = r1[4 * y : 4 * y + 4]
                out[y, tile, width : width + 128] = folded[(2 * y - 1) % 16]
                out[y, tile, width + 128 : width + 256] = folded[(2 * y + 2) % 16]


def front_kernel(scal, *refs):
    pack_kernel(*refs[0:6], *refs[12:14])
    press_kernel(scal, *refs[6:12], refs[14])


def front(scal, air_now, air_prev, plate_now, plate_prev):
    depth, height, width = air_now.shape
    rows, cols = plate_now.shape
    low = pl.BlockSpec((depth, 8, width), lambda i, *scal: (0, 0, 0))
    high = pl.BlockSpec((depth, 8, width), lambda i, *scal: (0, height // 8 - 1, 0))
    plate = pl.BlockSpec((rows, cols), lambda i, *scal: (0, 0))
    pack = pl.BlockSpec((8, cols + 2 * width), lambda i, *scal: (0, 0))

    def plane(offset):
        def where(k, *scal):
            scal = Place(*scal)
            return (jnp.clip(scal[0] + offset - scal[2], 0, depth - 1), 0, 0)

        return pl.BlockSpec((1, height, width), where)

    return pl.pallas_call(
        placed(front_kernel),
        grid_spec=pltpu.PrefetchScalarGridSpec(
            num_scalar_prefetch=2,
            grid=(1,),
            in_specs=[low, high, low, high, plate, plate]
            + [plane(2), plane(1), plane(0), plane(-1), plane(1), plane(0)],
            out_specs=[pack, pack]
            + [pl.BlockSpec((8, 32, width + 256), lambda k, *scal: (0, 0, 0))],
        ),
        out_shape=[jax.ShapeDtypeStruct((8, cols + 2 * width), F32)] * 2
        + [jax.ShapeDtypeStruct((8, 32, width + 256), F32)],
        compiler_params=params(59),
        cost_estimate=cost(6 << 20),
    )(
        *scal,
        *(air_now, air_now, air_prev, air_prev, plate_now, plate_prev),
        *(air_now, air_now, air_now, air_now, air_prev, air_prev),
    )


def flat_laplace(x):
    height = x.shape[0]
    return left_right(x) + pltpu.roll(x, 1, 0) + pltpu.roll(x, height - 1, 0) - 4.0 * x


def inside_rows(shape, first, last_row):
    row = iota(shape, 0) + first
    return (row >= 0) & (row < last_row)


def plate_step(ext, old, ok):
    inner = jnp.where(ok, flat_laplace(ext), 0.0)
    bend = flat_laplace(inner)
    return (2.0 * ext - 0.99 * old - 0.04 * bend) * (1.0 / 1.01)


def plate_kernel(n_rows, scal, now, prev, motion):
    rows, cols = now.shape
    first = scal[3] * rows - 4
    here = now[...]
    far = jnp.zeros((4, cols), F32)
    ext = jnp.concatenate([far, here, far], axis=0)
    old = jnp.concatenate([far, prev[...], far], axis=0)
    ok = inside_rows(ext.shape, first, n_rows)
    nxt = jnp.where(ok, plate_step(ext, old, ok), 0.0) - ext
    both = jnp.concatenate([here - prev[...], nxt], axis=0)
    fold = jnp.where((iota((512, 128), 0) >> 2) == iota((512, 128), 1), 1.0, 0.0)
    parts = [
        jnp.dot(both[:, 512 * q : 512 * q + 512], fold, precision=HIGH, preferred_element_type=F32)
        for q in range(cols // 512)
    ]
    narrow = jnp.concatenate(parts, axis=1)
    width = narrow.shape[1]
    row = iota((16, 40), 0)
    source = jnp.where(row < 4, row, jnp.where(row < 8, row + 1, jnp.where(row == 8, 4, 9)))
    pick = jnp.where((source == (iota((16, 40), 1) >> 2)) & (row < 10), 1.0 / 16.0, 0.0)
    lines = jnp.dot(pick, narrow, precision=HIGH, preferred_element_type=F32)
    motion[:, 0:width] = lines[0:8]
    motion[:, width : width + 128] = fold_row(lines[8:9])
    motion[:, width + 128 : width + 256] = fold_row(lines[9:10])


def plate_first(scal, now, prev, n_rows):
    rows, cols = now.shape
    return pl.pallas_call(
        placed(functools.partial(plate_kernel, n_rows)),
        in_specs=[pl.BlockSpec(memory_space=pltpu.SMEM)] * 2
        + [pl.BlockSpec(memory_space=pltpu.VMEM)] * 2,
        out_specs=pl.BlockSpec(memory_space=pltpu.VMEM),
        out_shape=jax.ShapeDtypeStruct((8, cols // 4 + 256), F32),
        compiler_params=params(16),
        cost_estimate=cost(4 << 20),
    )(*scal, now, prev)


def carries(shape, strip, b):
    return (4 * strip + (iota(shape, 0) & 3) + b) >= 32


def to_plate_kernel(scal, came, motion, out):
    shift, strip = scal[1], scal[4]
    a, b = shift >> 5, shift & 31
    move = motion[...]
    width = move.shape[1] - 256
    carry = carries((8, width), strip, b)
    before = (4 * strip - 1 + b) >> 5
    behind = (4 * strip + 4 + b) >> 5

    def folded(block, lane):
        ok = jnp.where((block >= 0) & (block < 32), 1.0, 0.0).astype(F32)
        at = pl.multiple_of(8 * jnp.clip(block, 0, 31), 8)
        return came[pl.ds(at, 8), lane : lane + 128] * ok

    slab = scal[5]
    pair = jnp.clip((scal[0] - 1) >> 3, 0, 14)
    aside = (slab < pair) | (slab > pair + 1)
    for dest in range(16):
        at = pl.multiple_of(8 * (dest + a), 8)
        after = pl.multiple_of(8 * jnp.minimum(dest + a + 1, 31), 8)
        tile = jnp.where(carry, came[pl.ds(after, 8), 0:width], came[pl.ds(at, 8), 0:width])
        wants = aside & ((pair == dest) | (pair + 1 == dest))
        out[dest, :, 0:width] = jnp.where(wants, move[:, 0:width], tile)
        for n, block in ((0, dest + a + before), (1, dest + a + behind)):
            lane = width + 128 * n
            part = folded(block, lane)
            out[dest, :, lane : lane + 128] = jnp.where(wants, move[:, lane : lane + 128], part)


def to_plate(scal, came, motion):
    width = motion.shape[1] - 256
    return pl.pallas_call(
        placed(to_plate_kernel),
        in_specs=[pl.BlockSpec(memory_space=pltpu.SMEM)] * 2
        + [pl.BlockSpec(memory_space=pltpu.VMEM)] * 2,
        out_specs=pl.BlockSpec(memory_space=pltpu.VMEM),
        out_shape=jax.ShapeDtypeStruct((16, 8, width + 256), F32),
        compiler_params=params(16),
        cost_estimate=cost(2 << 20),
    )(*scal, came, motion)


def to_air_kernel(scal, came, motion, on_chip, off_chip, pressure, out, moves):
    shift, strip, slab = scal[1], scal[4], scal[5]
    a, b = shift >> 5, shift & 31
    width = pressure.shape[1] - 256
    pair = jnp.clip((scal[0] - 1) >> 3, 0, 14)
    pressure[...] = came[pair] + came[pair + 1]
    for src in range(16):
        moves[src] = came[src]
    moves[slab] = motion[...]
    moves[slab ^ 1] = on_chip[...]

    @pl.when((slab > 0) & (slab < 15))
    def _():
        moves[jnp.where((slab & 1) == 0, slab - 1, slab + 1)] = off_chip[...]

    shape = (8, width)
    carry = carries(shape, strip, b)
    row = iota(shape, 0)
    place = (4 * strip + (row & 3) + b) & 31
    first_field = row < 4
    before = (4 * strip - 1 + b) >> 5
    behind = (4 * strip + 4 + b) >> 5

    def part(src, lanes):
        ok = jnp.where((src >= 0) & (src < 16), 1.0, 0.0).astype(F32)
        return moves[jnp.clip(src, 0, 15), :, lanes] * ok

    def tile(block):
        lanes = slice(0, width)
        return jnp.where(carry, part(block - a - 1, lanes), part(block - a, lanes))

    def rim(block, spot):
        rows = jnp.where(first_field & (place == spot), tile(block), 0.0)
        return fold_row(jnp.sum(rows, axis=0, keepdims=True))

    none = jnp.zeros((8, 128), F32)
    for s in range(8):
        for k in range(4):
            at = slice(8 * k, 8 * k + 8)
            block = 4 * s + k
            out[s, at, 0:width] = tile(block)
            lanes = slice(width, width + 128)
            out[s, at, lanes] = part(block - a - before, lanes)
            lanes = slice(width + 128, width + 256)
            out[s, at, lanes] = part(block - a - behind, lanes)
        lanes = slice(width + 256, width + 384)
        out[s, 0:8, lanes] = rim(4 * s - 1, 31) if s > 0 else none
        out[s, 8:16, lanes] = rim(4 * s + 4, 0) if s < 7 else none
        out[s, 16:24, lanes] = none
        out[s, 24:32, lanes] = none


def to_air(scal, came, motion, on_chip, off_chip):
    width = motion.shape[1] - 256
    return pl.pallas_call(
        placed(to_air_kernel),
        in_specs=[pl.BlockSpec(memory_space=pltpu.SMEM)] * 2
        + [pl.BlockSpec(memory_space=pltpu.VMEM)] * 4,
        out_specs=[pl.BlockSpec(memory_space=pltpu.VMEM)] * 2,
        out_shape=[
            jax.ShapeDtypeStruct((8, width + 256), F32),
            jax.ShapeDtypeStruct((8, 32, width + 384), F32),
        ],
        scratch_shapes=[pltpu.VMEM((16, 8, width + 256), F32)],
        compiler_params=params(16),
        cost_estimate=cost(2 << 20),
    )(*scal, came, motion, on_chip, off_chip)


def add_corner_kernel(scal, field, on_chip, off_chip, out):
    t = pl.program_id(0)
    lower_core = (scal[5] & 1) == 0
    low = t < 2
    first_end = (t & 1) == 0
    near = jnp.where(jnp.logical_not(jnp.logical_xor(low, lower_core)), off_chip[...], on_chip[...])
    line = jnp.where(first_end, near[0:1], near[1:2])
    row = iota(out.shape[1:], 0)
    spot = jnp.where(first_end, 0, 7)
    out[0] = field[0] + jnp.where(row == spot, 0.18 * line, 0.0)


def add_corners(scal, field, on_chip, off_chip):
    depth, height, width = field.shape

    def where(t, *scal):
        return ((t >> 1) * (depth - 1), (t & 1) * (height // 8 - 1), 0)

    tile = pl.BlockSpec((1, 8, width), where)
    pack = pl.BlockSpec((8, width), lambda t, *scal: (0, 0))
    return pl.pallas_call(
        placed(add_corner_kernel),
        grid_spec=pltpu.PrefetchScalarGridSpec(
            num_scalar_prefetch=2, grid=(4,), in_specs=[tile, pack, pack], out_specs=tile
        ),
        out_shape=jax.ShapeDtypeStruct(field.shape, F32),
        input_output_aliases={2: 0},
        compiler_params=params(59),
        cost_estimate=cost(1 << 20),
    )(*scal, field, on_chip, off_chip)


def force_kernel(scal, field, came, press, out, q, r):
    level, shift, base = scal[0], scal[1], scal[2]
    t = pl.program_id(0)
    height, width = q.shape
    depth = 8
    b = shift & 31

    @pl.when(t == 0)
    def _():
        for k in range(height // 32):
            at = slice(32 * k, 32 * k + 32)
            tiles = [came[y, 8 * k : 8 * k + 8, :] for y in range(8)]
            now = jnp.concatenate([x[0:4, 0:width] for x in tiles], axis=0)
            later = []
            for y in range(8):
                own = tiles[y][4:8, 0:width]
                row = iota(own.shape, 0)
                top = unfold(tiles[(y - 1) % 8][:, width + 128 : width + 256])
                bottom = unfold(tiles[(y + 1) % 8][:, width : width + 128])
                own = own + jnp.where(row == 0, top, 0.0) + jnp.where(row == 3, bottom, 0.0)
                later.append(own)
            r[at, :] = pltpu.roll(now, b, 0)
            q[at, :] = pltpu.roll(jnp.concatenate(later, axis=0), b, 0)
        rim = came[0, 0:16, width + 256 : width + 384]
        for y in range(1, 8):
            rim = rim + came[y, 0:16, width + 256 : width + 384]
        above, below = unfold(rim[0:8]), unfold(rim[8:16])
        motion = r[...]
        around = left_right(motion) + up_down(motion, above, below)
        q[...] = (0.55 - 0.6) * motion + 0.15 * around + 0.5 * q[...] + press[...]

    z = jnp.clip(level - 1 + t - base, 0, depth - 1) + base

    def is_level(other):
        return jnp.where(z == other, 1.0, 0.0).astype(F32)

    wq = is_level(level) - is_level(level + 1)
    wr = 0.15 * (is_level(level - 1) - is_level(level + 2))
    out[0] = field[0] + wq * q[...] + wr * r[...]


def add_force(scal, field, came, press):
    depth, height, width = field.shape

    def where(t, *scal):
        scal = Place(*scal)
        return (jnp.clip(scal[0] - 1 + t - scal[2], 0, depth - 1), 0, 0)

    plane = pl.BlockSpec((1, height, width), where)
    return pl.pallas_call(
        placed(force_kernel),
        grid_spec=pltpu.PrefetchScalarGridSpec(
            num_scalar_prefetch=2,
            grid=(4,),
            in_specs=[
                plane,
                pl.BlockSpec((8, 32, width + 384), lambda t, *scal: (0, 0, 0)),
                pl.BlockSpec((height, width), lambda t, *scal: (0, 0)),
            ],
            out_specs=plane,
            scratch_shapes=[pltpu.VMEM((height, width), F32)] * 2,
        ),
        out_shape=jax.ShapeDtypeStruct(field.shape, F32),
        input_output_aliases={2: 0},
        compiler_params=params(24),
        cost_estimate=cost(4 << 20),
    )(*scal, field, came, press)


def plate_last_kernel(n_rows, scal, now, prev, below, above, pressure, motion, out):
    rows, cols = now.shape
    first = scal[3] * rows - 4
    width = motion.shape[1] - 256
    press = pressure[0:4, 0:width]
    lo = unfold(pressure[:, width : width + 128])
    hi = unfold(pressure[:, width + 128 : width + 256])
    around = left_right(press) + up_down(press, lo, hi) - 4.0 * press
    later = 2.0 * press + 0.3 * around + pressure[4:8, 0:width] - motion[0:4, 0:width]
    lines = jnp.concatenate([press, later, lo, hi, jnp.zeros((6, width), F32)], axis=0)
    spread = jnp.where((iota((128, 512), 1) >> 2) == iota((128, 512), 0), 1.0, 0.0)
    parts = [
        jnp.dot(lines[:, 128 * q : 128 * q + 128], spread, precision=HIGH, preferred_element_type=F32)
        for q in range(width // 128)
    ]
    wide = jnp.concatenate(parts, axis=1)
    e = iota((24, 16), 0)
    line = iota((24, 16), 1)
    source = jnp.where(e < 4, 8, jnp.where(e >= 20, 9, (e - 4) >> 2))
    pick = jnp.where(line == source, C_PRESS, 0.0)
    push = jnp.dot(pick, wide, precision=HIGH, preferred_element_type=F32)
    pick = jnp.where(iota((16, 16), 1) == 4 + (iota((16, 16), 0) >> 2), C_PRESS, 0.0)
    push_last = jnp.dot(pick, wide, precision=HIGH, preferred_element_type=F32)
    here = now[...]
    ext = jnp.concatenate([below[0:4, 0:cols], here, above[0:4, 0:cols]], axis=0)
    old = jnp.concatenate([below[4:8, 0:cols], prev[...], above[4:8, 0:cols]], axis=0)
    ok = inside_rows(ext.shape, first, n_rows)
    mid = jnp.where(ok, plate_step(ext, old, ok) + push, 0.0)
    inner = jnp.where(ok, flat_laplace(mid), 0.0)
    bend = flat_laplace(inner)[4 : 4 + rows]
    final = (2.0 * mid[4 : 4 + rows] - 0.99 * here - 0.04 * bend) * (1.0 / 1.01)
    out[...] = final + push_last


def plate_last(scal, now, prev, lo, hi, pressure, motion, n_rows):
    return pl.pallas_call(
        placed(functools.partial(plate_last_kernel, n_rows)),
        in_specs=[pl.BlockSpec(memory_space=pltpu.SMEM)] * 2
        + [pl.BlockSpec(memory_space=pltpu.VMEM)] * 6,
        out_specs=pl.BlockSpec(memory_space=pltpu.VMEM),
        out_shape=jax.ShapeDtypeStruct(now.shape, F32),
        compiler_params=params(16),
        cost_estimate=cost(4 << 20),
    )(*scal, now, prev, lo, hi, pressure, motion)


def neighbours(n):
    return [(i, i + 1) for i in range(n - 1)], [(i + 1, i) for i in range(n - 1)]


def shards(air_now, air_prev, plate_now, plate_prev, plate_level, plate_shift):
    depth, height, width = air_now.shape
    n_gz, n_gy = lax.axis_size("gz"), lax.axis_size("gy")
    n_rows = plate_now.shape[0] * n_gz * n_gy
    cols = plate_now.shape[1]
    scal = (plate_level, plate_shift)
    up_d, down_d = neighbours(n_gz * n_gy)

    first, last, sent = front(scal, air_now, air_prev, plate_now, plate_prev)
    came = lax.all_to_all(sent, "gy", 0, 0).reshape(256, width + 256)
    lo = lax.ppermute(last, ("gz", "gy"), up_d)
    hi = lax.ppermute(first, ("gz", "gy"), down_d)

    across = [(i, i + 1) for i in range(1, n_gz - 1, 2)]
    pairs_on = [(i, i ^ 1) for i in range(n_gz)]
    pairs_off = across + [(j, i) for i, j in across]
    motion = plate_first(scal, plate_now, plate_prev, n_rows)
    motion_on = lax.ppermute(motion, "gz", pairs_on)
    motion_off = lax.ppermute(motion, "gz", pairs_off)
    level, motion_on, motion_off = lax.optimization_barrier((plate_level, motion_on, motion_off))
    on_chip, off_chip = faces((level, plate_shift), air_now, air_prev)
    motion, on_chip, off_chip = lax.optimization_barrier((motion, on_chip, off_chip))
    on_chip = lax.ppermute(on_chip, "gz", pairs_on)
    off_chip = lax.ppermute(off_chip, "gz", pairs_off)

    came = lax.all_to_all(to_plate(scal, came, motion), "gz", 0, 0)
    came, lo, hi, on_chip, off_chip = lax.optimization_barrier((came, lo, hi, on_chip, off_chip))
    corner_on, corner_off = corners(scal, lo, hi, cols, width)
    corner_on = lax.ppermute(corner_on, "gz", pairs_on)
    corner_off = lax.ppermute(corner_off, "gz", pairs_off)
    pressure, sent = to_air(scal, came, motion, motion_on, motion_off)
    air_2, press_now = air_steps(
        scal, air_now, air_prev, on_chip, off_chip, lo, hi, cols
    )
    came = lax.all_to_all(sent, "gy", 0, 0)

    plate_2 = plate_last(scal, plate_now, plate_prev, lo, hi, pressure, motion, n_rows)
    air_2 = add_corners(scal, air_2, corner_on, corner_off)
    air_2 = add_force(scal, air_2, came, press_now)
    return (air_2, plate_2)


def solution(mesh):
    in_specs = (
        P("gz", "gy", None),
        P("gz", "gy", None),
        P(("gz", "gy"), None),
        P(("gz", "gy"), None),
        P(),
        P(),
    )
    out_specs = (P("gz", "gy", None), P(("gz", "gy"), None))
    return jax.shard_map(shards, mesh=mesh, in_specs=in_specs, out_specs=out_specs, check_vma=False)
```

```python
import functools

import jax
import jax.numpy as jnp
from jax import lax
from jax.experimental import pallas as pl
from jax.experimental.pallas import tpu as pltpu
from jax.sharding import PartitionSpec as P

F32 = jnp.float32
C_PRESS = 0.5 / 1.01
HIGH = lax.Precision.HIGHEST


def params(mib):
    return pltpu.CompilerParams(vmem_limit_bytes=mib << 20)


class Place:
    def __init__(self, level, shift):
        self.level, self.shift = level, shift

    def __getitem__(self, i):
        if i == 0:
            return self.level[0]
        if i == 1:
            return self.shift[0]
        slab, strip = lax.axis_index("gz"), lax.axis_index("gy")
        return {2: slab * 8, 3: slab * lax.axis_size("gy") + strip, 4: strip, 5: slab}[i]


def placed(kernel):
    def run(level, shift, *refs):
        kernel(Place(level, shift), *refs)

    return run


def cost(nbytes):
    return pl.CostEstimate(flops=nbytes, bytes_accessed=nbytes, transcendentals=0)


def iota(shape, axis):
    return lax.broadcasted_iota(jnp.int32, shape, axis)


def left_right(x):
    width = x.shape[1]
    col = iota(x.shape, 1)
    west = jnp.where(col == 0, 0.0, pltpu.roll(x, 1, 1))
    east = jnp.where(col == width - 1, 0.0, pltpu.roll(x, width - 1, 1))
    return west + east


def up_down(x, above, below):
    height = x.shape[0]
    row = iota(x.shape, 0)
    up = jnp.where(row == 0, above, pltpu.roll(x, 1, 0))
    down = jnp.where(row == height - 1, below, pltpu.roll(x, height - 1, 0))
    return up + down


def sweep(load, count, above, below, emit):
    here = load(0)
    shape = here.shape
    width = shape[1]
    row, col = iota(shape, 0), iota(shape, 1)
    top, bottom, left, right = row == 0, row == 7, col == 0, col == width - 1
    from_above = above
    up, down = pltpu.roll(here, 1, 0), pltpu.roll(here, 7, 0)
    for i in range(count):
        if i + 1 < count:
            later = load(i + 1)
            later_up, later_down = pltpu.roll(later, 1, 0), pltpu.roll(later, 7, 0)
            from_below = later_down
        else:
            from_below = below
        west = jnp.where(left, 0.0, pltpu.roll(here, 1, 1))
        east = jnp.where(right, 0.0, pltpu.roll(here, width - 1, 1))
        vertical = jnp.where(top, from_above, up) + jnp.where(bottom, from_below, down)
        emit(i, here, west + east + vertical)
        if i + 1 < count:
            from_above = up
            here, up, down = later, later_up, later_down


def pack_kernel(now0, now1, old0, old1, plate_now, plate_prev, first, last):
    rows = plate_now.shape[0]
    cols = plate_now.shape[1]
    width = now0.shape[2]
    for out, now, old, edge, inner, r in (
        (first, now0, old0, 0, 1, 0),
        (last, now1, old1, 7, 6, rows - 4),
    ):
        here = now[:, edge, :]
        depth = here.shape[0]
        out[0:4, 0:cols] = plate_now[r : r + 4, :]
        out[4:8, 0:cols] = plate_prev[r : r + 4, :]
        out[:, cols : cols + width] = here
        around = left_right(here) + up_down(here, 0.0, 0.0) + now[:, inner, :]
        out[:, cols + width : cols + 2 * width] = 0.2 * here - old[:, edge, :] + 0.3 * around


def face_kernel(scal, here, inner, old, on_chip, off_chip):
    height = here.shape[1]

    def one(out):
        def emit(i, x, around):
            at = slice(8 * i, 8 * i + 8)
            out[at, :] = x
            part = 0.2 * x - old[0, at, :] + 0.3 * (around + inner[0, at, :])
            out[height + 8 * i : height + 8 * i + 8, :] = part

        sweep(lambda i: here[0, 8 * i : 8 * i + 8, :], height // 8, 0.0, 0.0, emit)

    @pl.when(pl.program_id(0) == 0)
    def _():
        one(on_chip)

    @pl.when(pl.program_id(0) == 1)
    def _():
        one(off_chip)


def faces(scal, air_now, air_prev):
    depth, height, width = air_now.shape

    def plane(inner):
        def where(i, *scal):
            top = ((Place(*scal)[5] + i) & 1) == 0
            return (jnp.where(top, depth - 1 - inner, inner), 0, 0)

        return pl.BlockSpec((1, height, width), where)

    out = pl.BlockSpec((2 * height, width), lambda i, *scal: (0, 0))
    return pl.pallas_call(
        placed(face_kernel),
        grid_spec=pltpu.PrefetchScalarGridSpec(
            num_scalar_prefetch=2,
            grid=(2,),
            in_specs=[
                plane(0),
                plane(1),
                plane(0),
            ],
            out_specs=[out, out],
        ),
        out_shape=[jax.ShapeDtypeStruct((2 * height, width), F32)] * 2,
        compiler_params=params(59),
        cost_estimate=cost(5 << 20),
    )(*scal, air_now, air_now, air_prev)


def corner_kernel(scal, lo, hi, on_chip, off_chip):
    strip = scal[4]
    lower_core = (scal[5] & 1) == 0
    row = iota(on_chip.shape, 0)

    def ends(level):
        above = jnp.where(strip > 0, lo[level : level + 1, :], 0.0)
        below = jnp.where(strip < 7, hi[level : level + 1, :], 0.0)
        return jnp.where(row == 0, above, jnp.where(row == 1, below, 0.0))

    bottom, top = ends(0), ends(7)
    on_chip[...] = jnp.where(lower_core, top, bottom)
    off_chip[...] = jnp.where(lower_core, bottom, top)


def corners(scal, lo, hi, cols, width):
    edge = pl.BlockSpec((8, width), lambda i, *scal: (0, cols // width))
    out = pl.BlockSpec((8, width), lambda i, *scal: (0, 0))
    return pl.pallas_call(
        placed(corner_kernel),
        grid_spec=pltpu.PrefetchScalarGridSpec(
            num_scalar_prefetch=2, grid=(1,), in_specs=[edge, edge], out_specs=[out, out]
        ),
        out_shape=[jax.ShapeDtypeStruct((8, width), F32)] * 2,
        compiler_params=params(16),
        cost_estimate=cost(1 << 20),
    )(*scal, lo, hi)


def air_kernel(
    scal, now, prev, on_chip, off_chip, ylo, yhi,
    out, press, keep, mid, older, sems,
):
    level, shift, first, strip, slab = scal[0], scal[1], scal[2], scal[4], scal[5]
    t = pl.program_id(0)
    depth, height, width = now.shape
    strips = [slice(8 * i, 8 * i + 8) for i in range(height // 8)]
    y_lo = jnp.where(strip > 0, 1.0, 0.0).astype(F32)
    y_hi = jnp.where(strip < 7, 1.0, 0.0).astype(F32)
    lower_core = (slab & 1) == 0

    def zlo(first, count):
        at = slice(first, first + count)
        return jnp.where(lower_core, off_chip[at, :], on_chip[at, :])

    def zhi(first, count):
        at = slice(first, first + count)
        return jnp.where(lower_core, on_chip[at, :], off_chip[at, :])

    def fetch_now(z):
        return pltpu.make_async_copy(now.at[z], keep.at[z + 1], sems.at[0, z])

    def fetch_prev(z):
        return pltpu.make_async_copy(prev.at[z], older.at[z], sems.at[1, z])

    @pl.when(t == 0)
    def _():
        for z in range(depth):
            fetch_now(z).start()
            fetch_prev(z).start()

    pairs = depth // 2

    @pl.when(t == 0)
    def _():
        fetch_now(0).wait()

    @pl.when(t < pairs)
    def _():
        fetch_now(2 * t + 1).wait()
        fetch_prev(2 * t).wait()
        fetch_prev(2 * t + 1).wait()

    @pl.when(t < pairs - 1)
    def _():
        fetch_now(2 * t + 2).wait()

    def outer(target, source, level, inside):
        inside = jnp.where(inside, 1.0, 0.0).astype(F32)
        for i, at in enumerate(strips):
            mid[target, at, :] = inside * (source(height + 8 * i, 8) + 0.3 * keep[level, at, :])

    @pl.when(t == 0)
    def _():
        for i, at in enumerate(strips):
            keep[0, at, :] = zlo(8 * i, 8)
            keep[depth + 1, at, :] = zhi(8 * i, 8)
        outer(0, zlo, 1, slab > 0)

    @pl.when(t == pairs - 1)
    def _():
        outer(depth + 1, zhi, depth, slab < 15)

    def first_step(z):
        above = y_lo * ylo[pl.ds(z, 1), 0:width]
        below = y_hi * yhi[pl.ds(z, 1), 0:width]

        def emit(i, x, around):
            at = strips[i]
            total = around + keep[z, at, :] + keep[z + 2, at, :]
            mid[z + 1, at, :] = 0.2 * x - older[z, at, :] + 0.3 * total

        sweep(lambda i: keep[z + 1, strips[i], :], len(strips), above, below, emit)

    def second_step(z, slot):
        def rim(rows, line):
            return rows[pl.ds(z, 1), width : 2 * width] + 0.3 * line

        above = y_lo * rim(ylo, keep[z + 1, 0:1, :])
        below = y_hi * rim(yhi, keep[z + 1, height - 1 : height, :])

        def emit(i, x, around):
            at = strips[i]
            total = around + mid[z, at, :] + mid[z + 2, at, :]
            out[slot, at, :] = 0.2 * x - keep[z + 1, at, :] + 0.3 * total

        sweep(lambda i: mid[z + 1, strips[i], :], len(strips), above, below, emit)

    @pl.when(t < pairs)
    def _():
        first_step(2 * t)
        first_step(2 * t + 1)

    @pl.when(t >= 1)
    def _():
        second_step(2 * t - 2, 0)
        second_step(2 * t - 1, 1)

    @pl.when(t == pairs)
    def _():
        upper = jnp.clip(level + 1 - first, -1, depth) + 1
        lower = jnp.clip(level - first, -1, depth) + 1
        for i, at in enumerate(strips):
            y = iota((8, width), 0) + (strip * height + 8 * i - shift)
            gap = keep[upper, at, :] - keep[lower, at, :]
            press[at, :] = jnp.where((y >= 0) & (y < 512), (0.5 * C_PRESS) * gap, 0.0)


def air_steps(scal, now, prev, on_chip, off_chip, ylo, yhi, cols):
    depth, height, width = now.shape

    pair = pl.BlockSpec(
        (2, height, width), lambda t, *scal: (jnp.clip(t - 1, 0, depth // 2 - 1), 0, 0)
    )
    whole = pl.BlockSpec(memory_space=pl.ANY)

    z_face = pl.BlockSpec((2 * height, width), lambda t, *scal: (0, 0))
    rows = pl.BlockSpec((8, 2 * width), lambda t, *scal: (0, cols // (2 * width)))
    return pl.pallas_call(
        placed(air_kernel),
        grid_spec=pltpu.PrefetchScalarGridSpec(
            num_scalar_prefetch=2,
            grid=(depth // 2 + 1,),
            in_specs=[whole, whole, z_face, z_face, rows, rows],
            out_specs=[
                pair,
                pl.BlockSpec((height, width), lambda t, *scal: (0, 0)),
            ],
            scratch_shapes=[pltpu.VMEM((depth + 2, height, width), F32)] * 2
            + [pltpu.VMEM(now.shape, F32), pltpu.SemaphoreType.DMA((2, depth))],
        ),
        out_shape=[
            jax.ShapeDtypeStruct(now.shape, F32),
            jax.ShapeDtypeStruct((height, width), F32),
        ],
        compiler_params=params(59),
        cost_estimate=cost(24 << 20),
    )(*scal, now, prev, on_chip, off_chip, ylo, yhi)


def fold_row(row):
    return jnp.concatenate([row[:, 128 * q : 128 * q + 128] for q in range(8)], axis=0)


def unfold(tile):
    return jnp.concatenate([tile[q : q + 1] for q in range(8)], axis=1)


def press_kernel(scal, up2, up1, at0, dn1, pup1, pat0, out):
    level, shift, base = scal[0], scal[1], scal[2]
    depth = 8
    width = up1.shape[2]

    def mine(z):
        return jnp.where((z >= base) & (z < base + depth), 1.0, 0.0).astype(F32)

    here = (level + 2 >= base) & (level - 1 < base + depth)

    @pl.when(jnp.logical_not(here))
    def _():
        out[...] = jnp.zeros(out.shape, F32)

    @pl.when(here)
    def _():
        m1, m0 = mine(level + 1), mine(level)
        m2, mm = mine(level + 2), mine(level - 1)
        b = shift & 31
        turn = (32 - b) & 31
        for k in range(up1.shape[1] // 32):
            at = slice(32 * k, 32 * k + 32)
            press = m1 * up1[0, at, :] - m0 * at0[0, at, :]
            vertical = m2 * up2[0, at, :] - 3.0 * press - mm * dn1[0, at, :]
            older = m1 * pup1[0, at, :] - m0 * pat0[0, at, :]
            r0 = pltpu.roll(press, turn, 0)
            r1 = pltpu.roll(0.3 * vertical - older, turn, 0)
            folded = [fold_row(r0[i : i + 1]) for i in range(32) if i & 3 in (0, 3)]
            for y in range(8):
                tile = slice(8 * k, 8 * k + 8)
                out[y, 8 * k : 8 * k + 4, 0:width] = r0[4 * y : 4 * y + 4]
                out[y, 8 * k + 4 : 8 * k + 8, 0:width] = r1[4 * y : 4 * y + 4]
                out[y, tile, width : width + 128] = folded[(2 * y - 1) % 16]
                out[y, tile, width + 128 : width + 256] = folded[(2 * y + 2) % 16]


def front_kernel(scal, *refs):
    pack_kernel(*refs[0:6], *refs[12:14])
    press_kernel(scal, *refs[6:12], refs[14])


def front(scal, air_now, air_prev, plate_now, plate_prev):
    depth, height, width = air_now.shape
    rows, cols = plate_now.shape
    low = pl.BlockSpec((depth, 8, width), lambda i, *scal: (0, 0, 0))
    high = pl.BlockSpec((depth, 8, width), lambda i, *scal: (0, height // 8 - 1, 0))
    plate = pl.BlockSpec((rows, cols), lambda i, *scal: (0, 0))
    pack = pl.BlockSpec((8, cols + 2 * width), lambda i, *scal: (0, 0))

    def plane(offset):
        def where(k, *scal):
            scal = Place(*scal)
            return (jnp.clip(scal[0] + offset - scal[2], 0, depth - 1), 0, 0)

        return pl.BlockSpec((1, height, width), where)

    return pl.pallas_call(
        placed(front_kernel),
        grid_spec=pltpu.PrefetchScalarGridSpec(
            num_scalar_prefetch=2,
            grid=(1,),
            in_specs=[low, high, low, high, plate, plate]
            + [plane(2), plane(1), plane(0), plane(-1), plane(1), plane(0)],
            out_specs=[pack, pack]
            + [pl.BlockSpec((8, 32, width + 256), lambda k, *scal: (0, 0, 0))],
        ),
        out_shape=[jax.ShapeDtypeStruct((8, cols + 2 * width), F32)] * 2
        + [jax.ShapeDtypeStruct((8, 32, width + 256), F32)],
        compiler_params=params(59),
        cost_estimate=cost(6 << 20),
    )(
        *scal,
        *(air_now, air_now, air_prev, air_prev, plate_now, plate_prev),
        *(air_now, air_now, air_now, air_now, air_prev, air_prev),
    )


def flat_laplace(x):
    height = x.shape[0]
    return left_right(x) + pltpu.roll(x, 1, 0) + pltpu.roll(x, height - 1, 0) - 4.0 * x


def inside_rows(shape, first, last_row):
    row = iota(shape, 0) + first
    return (row >= 0) & (row < last_row)


def plate_step(ext, old, ok):
    inner = jnp.where(ok, flat_laplace(ext), 0.0)
    bend = flat_laplace(inner)
    return (2.0 * ext - 0.99 * old - 0.04 * bend) * (1.0 / 1.01)


def plate_kernel(n_rows, scal, now, prev, motion):
    rows, cols = now.shape
    first = scal[3] * rows - 4
    here = now[...]
    far = jnp.zeros((4, cols), F32)
    ext = jnp.concatenate([far, here, far], axis=0)
    old = jnp.concatenate([far, prev[...], far], axis=0)
    ok = inside_rows(ext.shape, first, n_rows)
    nxt = jnp.where(ok, plate_step(ext, old, ok), 0.0) - ext
    both = jnp.concatenate([here - prev[...], nxt], axis=0)
    fold = jnp.where((iota((512, 128), 0) >> 2) == iota((512, 128), 1), 1.0, 0.0)
    parts = [
        jnp.dot(both[:, 512 * q : 512 * q + 512], fold, precision=HIGH, preferred_element_type=F32)
        for q in range(cols // 512)
    ]
    narrow = jnp.concatenate(parts, axis=1)
    width = narrow.shape[1]
    row = iota((16, 40), 0)
    source = jnp.where(row < 4, row, jnp.where(row < 8, row + 1, jnp.where(row == 8, 4, 9)))
    pick = jnp.where((source == (iota((16, 40), 1) >> 2)) & (row < 10), 1.0 / 16.0, 0.0)
    lines = jnp.dot(pick, narrow, precision=HIGH, preferred_element_type=F32)
    motion[:, 0:width] = lines[0:8]
    motion[:, width : width + 128] = fold_row(lines[8:9])
    motion[:, width + 128 : width + 256] = fold_row(lines[9:10])


def plate_first(scal, now, prev, n_rows):
    rows, cols = now.shape
    return pl.pallas_call(
        placed(functools.partial(plate_kernel, n_rows)),
        in_specs=[pl.BlockSpec(memory_space=pltpu.SMEM)] * 2
        + [pl.BlockSpec(memory_space=pltpu.VMEM)] * 2,
        out_specs=pl.BlockSpec(memory_space=pltpu.VMEM),
        out_shape=jax.ShapeDtypeStruct((8, cols // 4 + 256), F32),
        compiler_params=params(16),
        cost_estimate=cost(4 << 20),
    )(*scal, now, prev)


def carries(shape, strip, b):
    return (4 * strip + (iota(shape, 0) & 3) + b) >= 32


def to_plate_kernel(scal, came, motion, out):
    shift, strip = scal[1], scal[4]
    a, b = shift >> 5, shift & 31
    move = motion[...]
    width = move.shape[1] - 256
    carry = carries((8, width), strip, b)
    before = (4 * strip - 1 + b) >> 5
    behind = (4 * strip + 4 + b) >> 5

    def folded(block, lane):
        ok = jnp.where((block >= 0) & (block < 32), 1.0, 0.0).astype(F32)
        at = pl.multiple_of(8 * jnp.clip(block, 0, 31), 8)
        return came[pl.ds(at, 8), lane : lane + 128] * ok

    slab = scal[5]
    pair = jnp.clip((scal[0] - 1) >> 3, 0, 14)
    aside = (slab < pair) | (slab > pair + 1)
    for dest in range(16):
        at = pl.multiple_of(8 * (dest + a), 8)
        after = pl.multiple_of(8 * jnp.minimum(dest + a + 1, 31), 8)
        tile = jnp.where(carry, came[pl.ds(after, 8), 0:width], came[pl.ds(at, 8), 0:width])
        wants = aside & ((pair == dest) | (pair + 1 == dest))
        out[dest, :, 0:width] = jnp.where(wants, move[:, 0:width], tile)
        for n, block in ((0, dest + a + before), (1, dest + a + behind)):
            lane = width + 128 * n
            part = folded(block, lane)
            out[dest, :, lane : lane + 128] = jnp.where(wants, move[:, lane : lane + 128], part)


def to_plate(scal, came, motion):
    width = motion.shape[1] - 256
    return pl.pallas_call(
        placed(to_plate_kernel),
        in_specs=[pl.BlockSpec(memory_space=pltpu.SMEM)] * 2
        + [pl.BlockSpec(memory_space=pltpu.VMEM)] * 2,
        out_specs=pl.BlockSpec(memory_space=pltpu.VMEM),
        out_shape=jax.ShapeDtypeStruct((16, 8, width + 256), F32),
        compiler_params=params(16),
        cost_estimate=cost(2 << 20),
    )(*scal, came, motion)


def to_air_kernel(scal, came, motion, on_chip, off_chip, pressure, out, moves):
    shift, strip, slab = scal[1], scal[4], scal[5]
    a, b = shift >> 5, shift & 31
    width = pressure.shape[1] - 256
    pair = jnp.clip((scal[0] - 1) >> 3, 0, 14)
    pressure[...] = came[pair] + came[pair + 1]
    for src in range(16):
        moves[src] = came[src]
    moves[slab] = motion[...]
    moves[slab ^ 1] = on_chip[...]

    @pl.when((slab > 0) & (slab < 15))
    def _():
        moves[jnp.where((slab & 1) == 0, slab - 1, slab + 1)] = off_chip[...]

    shape = (8, width)
    carry = carries(shape, strip, b)
    row = iota(shape, 0)
    place = (4 * strip + (row & 3) + b) & 31
    first_field = row < 4
    before = (4 * strip - 1 + b) >> 5
    behind = (4 * strip + 4 + b) >> 5

    def part(src, lanes):
        ok = jnp.where((src >= 0) & (src < 16), 1.0, 0.0).astype(F32)
        return moves[jnp.clip(src, 0, 15), :, lanes] * ok

    def tile(block):
        lanes = slice(0, width)
        return jnp.where(carry, part(block - a - 1, lanes), part(block - a, lanes))

    def rim(block, spot):
        rows = jnp.where(first_field & (place == spot), tile(block), 0.0)
        return fold_row(jnp.sum(rows, axis=0, keepdims=True))

    none = jnp.zeros((8, 128), F32)
    for s in range(8):
        for k in range(4):
            at = slice(8 * k, 8 * k + 8)
            block = 4 * s + k
            out[s, at, 0:width] = tile(block)
            lanes = slice(width, width + 128)
            out[s, at, lanes] = part(block - a - before, lanes)
            lanes = slice(width + 128, width + 256)
            out[s, at, lanes] = part(block - a - behind, lanes)
        lanes = slice(width + 256, width + 384)
        out[s, 0:8, lanes] = rim(4 * s - 1, 31) if s > 0 else none
        out[s, 8:16, lanes] = rim(4 * s + 4, 0) if s < 7 else none
        out[s, 16:24, lanes] = none
        out[s, 24:32, lanes] = none


def to_air(scal, came, motion, on_chip, off_chip):
    width = motion.shape[1] - 256
    return pl.pallas_call(
        placed(to_air_kernel),
        in_specs=[pl.BlockSpec(memory_space=pltpu.SMEM)] * 2
        + [pl.BlockSpec(memory_space=pltpu.VMEM)] * 4,
        out_specs=[pl.BlockSpec(memory_space=pltpu.VMEM)] * 2,
        out_shape=[
            jax.ShapeDtypeStruct((8, width + 256), F32),
            jax.ShapeDtypeStruct((8, 32, width + 384), F32),
        ],
        scratch_shapes=[pltpu.VMEM((16, 8, width + 256), F32)],
        compiler_params=params(16),
        cost_estimate=cost(2 << 20),
    )(*scal, came, motion, on_chip, off_chip)


def add_corner_kernel(scal, field, on_chip, off_chip, out):
    lower_core = (scal[5] & 1) == 0
    first_end = pl.program_id(0) == 0
    depth = field.shape[0]
    row = iota(field.shape[1:], 0)
    spot = jnp.where(first_end, 0, 7)

    def line(near):
        return jnp.where(row == spot, 0.18 * jnp.where(first_end, near[0:1], near[1:2]), 0.0)

    below = line(jnp.where(lower_core, off_chip[...], on_chip[...]))
    above = line(jnp.where(lower_core, on_chip[...], off_chip[...]))
    out[0] = field[0] + below
    for z in range(1, depth - 1):
        out[z] = field[z]
    out[depth - 1] = field[depth - 1] + above


def add_corners(scal, field, on_chip, off_chip):
    depth, height, width = field.shape

    tile = pl.BlockSpec((depth, 8, width), lambda t, *scal: (0, t * (height // 8 - 1), 0))
    pack = pl.BlockSpec((8, width), lambda t, *scal: (0, 0))
    return pl.pallas_call(
        placed(add_corner_kernel),
        grid_spec=pltpu.PrefetchScalarGridSpec(
            num_scalar_prefetch=2, grid=(2,), in_specs=[tile, pack, pack], out_specs=tile
        ),
        out_shape=jax.ShapeDtypeStruct(field.shape, F32),
        input_output_aliases={2: 0},
        compiler_params=params(8),
        cost_estimate=cost(1 << 20),
    )(*scal, field, on_chip, off_chip)


def force_kernel(scal, field, came, press, out, q, r):
    level, shift, base = scal[0], scal[1], scal[2]
    t = pl.program_id(0)
    height, width = q.shape
    depth = 8
    b = shift & 31

    @pl.when(t == 0)
    def _():
        for k in range(height // 32):
            at = slice(32 * k, 32 * k + 32)
            tiles = [came[y, 8 * k : 8 * k + 8, :] for y in range(8)]
            now = jnp.concatenate([x[0:4, 0:width] for x in tiles], axis=0)
            later = []
            for y in range(8):
                own = tiles[y][4:8, 0:width]
                row = iota(own.shape, 0)
                top = unfold(tiles[(y - 1) % 8][:, width + 128 : width + 256])
                bottom = unfold(tiles[(y + 1) % 8][:, width : width + 128])
                own = own + jnp.where(row == 0, top, 0.0) + jnp.where(row == 3, bottom, 0.0)
                later.append(own)
            r[at, :] = pltpu.roll(now, b, 0)
            q[at, :] = pltpu.roll(jnp.concatenate(later, axis=0), b, 0)
        rim = came[0, 0:16, width + 256 : width + 384]
        for y in range(1, 8):
            rim = rim + came[y, 0:16, width + 256 : width + 384]
        above, below = unfold(rim[0:8]), unfold(rim[8:16])
        motion = r[...]
        around = left_right(motion) + up_down(motion, above, below)
        q[...] = (0.55 - 0.6) * motion + 0.15 * around + 0.5 * q[...] + press[...]

    z = jnp.clip(level - 1 + t - base, 0, depth - 1) + base

    def is_level(other):
        return jnp.where(z == other, 1.0, 0.0).astype(F32)

    wq = is_level(level) - is_level(level + 1)
    wr = 0.15 * (is_level(level - 1) - is_level(level + 2))
    out[0] = field[0] + wq * q[...] + wr * r[...]


def add_force(scal, field, came, press):
    depth, height, width = field.shape

    def where(t, *scal):
        scal = Place(*scal)
        return (jnp.clip(scal[0] - 1 + t - scal[2], 0, depth - 1), 0, 0)

    plane = pl.BlockSpec((1, height, width), where)
    return pl.pallas_call(
        placed(force_kernel),
        grid_spec=pltpu.PrefetchScalarGridSpec(
            num_scalar_prefetch=2,
            grid=(4,),
            in_specs=[
                plane,
                pl.BlockSpec((8, 32, width + 384), lambda t, *scal: (0, 0, 0)),
                pl.BlockSpec((height, width), lambda t, *scal: (0, 0)),
            ],
            out_specs=plane,
            scratch_shapes=[pltpu.VMEM((height, width), F32)] * 2,
        ),
        out_shape=jax.ShapeDtypeStruct(field.shape, F32),
        input_output_aliases={2: 0},
        compiler_params=params(24),
        cost_estimate=cost(4 << 20),
    )(*scal, field, came, press)


def plate_last_kernel(n_rows, scal, now, prev, below, above, pressure, motion, out):
    rows, cols = now.shape
    first = scal[3] * rows - 4
    width = motion.shape[1] - 256
    press = pressure[0:4, 0:width]
    lo = unfold(pressure[:, width : width + 128])
    hi = unfold(pressure[:, width + 128 : width + 256])
    around = left_right(press) + up_down(press, lo, hi) - 4.0 * press
    later = 2.0 * press + 0.3 * around + pressure[4:8, 0:width] - motion[0:4, 0:width]
    lines = jnp.concatenate([press, later, lo, hi, jnp.zeros((6, width), F32)], axis=0)
    spread = jnp.where((iota((128, 512), 1) >> 2) == iota((128, 512), 0), 1.0, 0.0)
    parts = [
        jnp.dot(lines[:, 128 * q : 128 * q + 128], spread, precision=HIGH, preferred_element_type=F32)
        for q in range(width // 128)
    ]
    wide = jnp.concatenate(parts, axis=1)
    e = iota((24, 16), 0)
    line = iota((24, 16), 1)
    source = jnp.where(e < 4, 8, jnp.where(e >= 20, 9, (e - 4) >> 2))
    pick = jnp.where(line == source, C_PRESS, 0.0)
    push = jnp.dot(pick, wide, precision=HIGH, preferred_element_type=F32)
    pick = jnp.where(iota((16, 16), 1) == 4 + (iota((16, 16), 0) >> 2), C_PRESS, 0.0)
    push_last = jnp.dot(pick, wide, precision=HIGH, preferred_element_type=F32)
    here = now[...]
    ext = jnp.concatenate([below[0:4, 0:cols], here, above[0:4, 0:cols]], axis=0)
    old = jnp.concatenate([below[4:8, 0:cols], prev[...], above[4:8, 0:cols]], axis=0)
    ok = inside_rows(ext.shape, first, n_rows)
    mid = jnp.where(ok, plate_step(ext, old, ok) + push, 0.0)
    inner = jnp.where(ok, flat_laplace(mid), 0.0)
    bend = flat_laplace(inner)[4 : 4 + rows]
    final = (2.0 * mid[4 : 4 + rows] - 0.99 * here - 0.04 * bend) * (1.0 / 1.01)
    out[...] = final + push_last


def plate_last(scal, now, prev, lo, hi, pressure, motion, n_rows):
    return pl.pallas_call(
        placed(functools.partial(plate_last_kernel, n_rows)),
        in_specs=[pl.BlockSpec(memory_space=pltpu.SMEM)] * 2
        + [pl.BlockSpec(memory_space=pltpu.VMEM)] * 6,
        out_specs=pl.BlockSpec(memory_space=pltpu.VMEM),
        out_shape=jax.ShapeDtypeStruct(now.shape, F32),
        compiler_params=params(16),
        cost_estimate=cost(4 << 20),
    )(*scal, now, prev, lo, hi, pressure, motion)


def neighbours(n):
    return [(i, i + 1) for i in range(n - 1)], [(i + 1, i) for i in range(n - 1)]


def shards(air_now, air_prev, plate_now, plate_prev, plate_level, plate_shift):
    depth, height, width = air_now.shape
    n_gz, n_gy = lax.axis_size("gz"), lax.axis_size("gy")
    n_rows = plate_now.shape[0] * n_gz * n_gy
    cols = plate_now.shape[1]
    scal = (plate_level, plate_shift)
    up_d, down_d = neighbours(n_gz * n_gy)

    first, last, sent = front(scal, air_now, air_prev, plate_now, plate_prev)
    came = lax.all_to_all(sent, "gy", 0, 0).reshape(256, width + 256)
    lo = lax.ppermute(last, ("gz", "gy"), up_d)
    hi = lax.ppermute(first, ("gz", "gy"), down_d)

    across = [(i, i + 1) for i in range(1, n_gz - 1, 2)]
    pairs_on = [(i, i ^ 1) for i in range(n_gz)]
    pairs_off = across + [(j, i) for i, j in across]
    motion = plate_first(scal, plate_now, plate_prev, n_rows)
    motion_on = lax.ppermute(motion, "gz", pairs_on)
    motion_off = lax.ppermute(motion, "gz", pairs_off)
    level, motion_on, motion_off = lax.optimization_barrier((plate_level, motion_on, motion_off))
    on_chip, off_chip = faces((level, plate_shift), air_now, air_prev)
    motion, on_chip, off_chip = lax.optimization_barrier((motion, on_chip, off_chip))
    on_chip = lax.ppermute(on_chip, "gz", pairs_on)
    off_chip = lax.ppermute(off_chip, "gz", pairs_off)

    came = lax.all_to_all(to_plate(scal, came, motion), "gz", 0, 0)
    came, lo, hi, on_chip, off_chip = lax.optimization_barrier((came, lo, hi, on_chip, off_chip))
    corner_on, corner_off = corners(scal, lo, hi, cols, width)
    corner_on = lax.ppermute(corner_on, "gz", pairs_on)
    corner_off = lax.ppermute(corner_off, "gz", pairs_off)
    pressure, sent = to_air(scal, came, motion, motion_on, motion_off)
    air_2, press_now = air_steps(
        scal, air_now, air_prev, on_chip, off_chip, lo, hi, cols
    )
    came = lax.all_to_all(sent, "gy", 0, 0)

    plate_2 = plate_last(scal, plate_now, plate_prev, lo, hi, pressure, motion, n_rows)
    air_2 = add_corners(scal, air_2, corner_on, corner_off)
    air_2 = add_force(scal, air_2, came, press_now)
    return (air_2, plate_2)


def solution(mesh):
    in_specs = (
        P("gz", "gy", None),
        P("gz", "gy", None),
        P(("gz", "gy"), None),
        P(("gz", "gy"), None),
        P(),
        P(),
    )
    out_specs = (P("gz", "gy", None), P(("gz", "gy"), None))
    return jax.shard_map(shards, mesh=mesh, in_specs=in_specs, out_specs=out_specs, check_vma=False)
```
